32 devices in a mesh: parts: 2 (over y), row: 4 (over z), col: 2 (over x), mode: 2 (over core).
Axes of the slice: x: 2, y: 2, z: 4, core: 2. Of those that a mesh axis runs over, the one named last changes fastest.
Arguments:
- obj: float32 [2, 1024, 512], P(None, ('parts', 'row'), 'col'), parts along dimension 1, may hold values from -5 to 5
- probe: float32 [2, 2, 256, 128], P('mode', None, 'parts'), parts along dimension 2, may hold values from -5 to 5
- positions: int32 [4, 2, 32, 2], P('row', 'col', 'parts'), parts along dimension 2, may hold values from -64 to 447, as said below
- counts: int32 [8, 2], P(('parts', 'row'), 'col'), parts along dimension 0, may hold values from 4 to 16, as said below
- measured: float32 [4, 2, 32, 128, 128], P('row', 'col', 'parts'), parts along dimension 2, may hold values from 0.1 to 6
Outputs:
- object_out: float32 [2, 1024, 512], P(None, ('parts', 'row'), 'col'), parts along dimension 1
- probe_out: float32 [2, 2, 256, 128], P('mode', None, 'parts'), parts along dimension 2
The draws below stay inside these ranges and needn't reach their ends.
There are 2 independent parts, one for each index of `parts`. The reference program is written for one: setup_inputs(seed, part) draws one part's arguments, and reference() takes and returns one part's arrays. A program takes and returns all parts, laid end to end along the dimension named above; each array names one. Nothing has to cross between parts.
Inputs may be any that keep to these rules, and one draw needn't show every extreme that they name: `positions`: position s of tile (r, c) has row in [r * 128 - 128//2, (r+1) * 128 - 128//2) and column in [c * 256 - 128//2, (c+1) * 256 - 128//2). `counts`: some tile has all 16 slots live.
All inputs are finite; a program needn't handle non-finite values.
Results may differ from the reference program's by a relative error of at most 0.0001.
Values sent between devices are 32-bit elements; how exact they have to be, the bound alone decides.
No kernel may reach another device: no remote copies, remote signals or barrier semaphores. Data moves between devices by JAX's collectives and lax.ppermute only.
A program may use at most 64 MiB of HBM per device.

```python
import math
import jax
import jax.numpy as jnp
from jax import lax

PROBE = 128
MODES = 2
TR = 128
TC = 256
P_DEV = 16
ITERS = 2
NR = 512
NC = 512
N_ROW = 4
N_COL = 2


def draw_positions(key, part):
    key = jax.random.fold_in(key, 11)
    first_key, second_key = jax.random.split(key)
    inner_rows = jax.random.randint(first_key, (N_ROW, N_COL, P_DEV), 0, TR, dtype=jnp.int32)
    inner_cols = jax.random.randint(second_key, (N_ROW, N_COL, P_DEV), 0, TC, dtype=jnp.int32)
    inner_rows = inner_rows.at[0, 0, 0].set(0).at[N_ROW - 1, N_COL - 1, P_DEV - 1].set(TR - 1)
    inner_cols = inner_cols.at[0, 0, 0].set(0).at[N_ROW - 1, N_COL - 1, P_DEV - 1].set(TC - 1)
    base_rows = jnp.arange(N_ROW, dtype=jnp.int32)[:, None, None] * TR - PROBE // 2
    base_cols = jnp.arange(N_COL, dtype=jnp.int32)[None, :, None] * TC - PROBE // 2
    return jnp.stack([inner_rows + base_rows, inner_cols + base_cols], axis=-1).astype(jnp.int32)


def draw_counts(key, part):
    key = jax.random.fold_in(key, 23)
    first_key, second_key = jax.random.split(key)
    tiles = N_ROW * N_COL
    lowest = max(1, P_DEV // 4)
    flat = jax.random.randint(first_key, (tiles,), lowest, P_DEV + 1, dtype=jnp.int32)
    chosen = jax.random.randint(second_key, (), 0, tiles, dtype=jnp.int32)
    flat = flat.at[chosen].set(P_DEV).at[(chosen + 1) % tiles].set(lowest)
    return flat.reshape(N_ROW, N_COL).astype(jnp.int32)


def level_of(key, shape, cuts, smallest, largest):
    def one(position, blocks):
        steps = jax.random.uniform(jax.random.fold_in(jax.random.fold_in(key, 6), position), (blocks,), jnp.float32, smallest / len(cuts), largest / len(cuts))
        return jnp.repeat(jnp.exp(steps), shape[position] // blocks).reshape((-1,) + (1,) * (len(shape) - position - 1))

    factor_of = one(*cuts[0])
    for cut in cuts[1:]:
        factor_of = factor_of * one(*cut)
    return factor_of


def scatter_about(own_key, extent, scale, limit, cuts=(), held_as=jnp.bfloat16):
    values = scale * jax.random.normal(own_key, extent, jnp.float32)
    if cuts:
        values = values * level_of(own_key, extent, cuts, -0.22, 0.18)
    return jnp.clip(values, -limit, limit).astype(held_as)


def setup_inputs(seed: int = 0, part: int = 0) -> dict:
    seeds = jax.random.split(jax.random.key(seed), 6)
    part_splits = jax.random.split(jax.random.fold_in(seeds[5], part), 6)
    return {
        "obj": scatter_about(part_splits[0], (2, NR, NC), 0.7, 5.0, ((1, 4), (2, 2)), jnp.float32),
        "probe": scatter_about(part_splits[1], (MODES, 2, PROBE, PROBE), 0.7, 5.0, ((0, 2),), jnp.float32),
        "positions": draw_positions(jax.random.fold_in(jax.random.fold_in(seeds[5], part), 71), part),
        "counts": draw_counts(jax.random.fold_in(jax.random.fold_in(seeds[5], part), 71), part),
        "measured": jnp.clip(jnp.exp(math.log(6.0) - 4.0943445 * jax.random.uniform(part_splits[4], (N_ROW, N_COL, P_DEV, PROBE, PROBE), jnp.float32) ** level_of(part_splits[4], (N_ROW, N_COL, P_DEV, PROBE, PROBE), ((0, 4), (1, 2)), -0.2, 0.2)), 0.1, 6.0),
    }


momentum = 0.5
object_rate = 0.1
probe_rate = 0.25

def forward_dft(real_part, imag_part):
    spectrum = jnp.fft.fft2(real_part + 1j * imag_part, norm='ortho')
    return (jnp.real(spectrum).astype(real_part.dtype), jnp.imag(spectrum).astype(real_part.dtype))

def inverse_dft(real_part, imag_part):
    spectrum = jnp.fft.ifft2(real_part + 1j * imag_part, norm='ortho')
    return (jnp.real(spectrum).astype(real_part.dtype), jnp.imag(spectrum).astype(real_part.dtype))

def block_terms(patches, probe_modes, measured_block, live_mask):
    probe_real = probe_modes[:, 0][None]
    probe_imag = probe_modes[:, 1][None]
    patch_real = patches[:, 0][:, None]
    patch_imag = patches[:, 1][:, None]
    wave_real = probe_real * patch_real - probe_imag * patch_imag
    wave_imag = probe_real * patch_imag + probe_imag * patch_real
    far_real, far_imag = forward_dft(wave_real, wave_imag)
    intensity = lax.optimization_barrier(jnp.sum(far_real * far_real + far_imag * far_imag, axis=1))
    weights = (1.0 - jnp.sqrt(measured_block) / jnp.sqrt(intensity + 1.0)) * live_mask[:, None, None]
    back_real, back_imag = inverse_dft(weights[:, None] * far_real, weights[:, None] * far_imag)
    object_real = lax.optimization_barrier(jnp.sum(probe_real * back_real + probe_imag * back_imag, axis=1))
    object_imag = lax.optimization_barrier(jnp.sum(probe_real * back_imag - probe_imag * back_real, axis=1))
    grad_real = lax.optimization_barrier(jnp.sum(patch_real * back_real + patch_imag * back_imag, axis=0))
    grad_imag = lax.optimization_barrier(jnp.sum(patch_real * back_imag - patch_imag * back_real, axis=0))
    return (jnp.stack([object_real, object_imag], axis=1), jnp.stack([grad_real, grad_imag], axis=1))

def gradients(current_object, current_probe, positions, counts, measured):
    half_probe = PROBE // 2
    padded = jnp.pad(current_object, ((0, 0), (half_probe, half_probe), (half_probe, half_probe)))
    offsets = (positions.reshape(N_ROW * N_COL, P_DEV, 2) + half_probe).astype(jnp.int32)
    measured_all = measured.reshape(N_ROW * N_COL, P_DEV, PROBE, PROBE)
    live_all = (jnp.arange(P_DEV, dtype=jnp.int32)[None, :] < counts.reshape(-1, 1)).astype(jnp.float32)

    def one_tile(carry, block):
        object_grad, probe_grad = carry
        tile_offsets, tile_measured, tile_live = block

        def cut(offset):
            return lax.dynamic_slice(padded, (jnp.int32(0), offset[0], offset[1]), (2, PROBE, PROBE))
        patches = jax.vmap(cut)(tile_offsets)
        pieces, tile_probe = block_terms(patches, current_probe, tile_measured, tile_live)

        def place(index, grad):
            offset = tile_offsets[index]
            corner = (jnp.int32(0), offset[0], offset[1])
            current = lax.dynamic_slice(grad, corner, (2, PROBE, PROBE))
            return lax.dynamic_update_slice(grad, current + pieces[index], corner)
        object_grad = lax.fori_loop(0, P_DEV, place, object_grad)
        return ((object_grad, probe_grad + tile_probe), None)
    start = (jnp.zeros_like(padded), jnp.zeros_like(current_probe))
    (object_grad, probe_grad), _ = lax.scan(one_tile, start, (offsets, measured_all, live_all))
    return (object_grad[:, half_probe:-half_probe, half_probe:-half_probe], probe_grad)

def reference(obj, probe, positions, counts, measured):
    prev_object, prev_probe = (obj, probe)
    cur_object, cur_probe = (obj, probe)
    probe_step = probe_rate / (P_DEV * N_ROW * N_COL)
    for iteration in range(ITERS):
        ahead_object = cur_object + momentum * (cur_object - prev_object)
        ahead_probe = cur_probe + momentum * (cur_probe - prev_probe)
        object_grad, probe_grad = gradients(ahead_object, ahead_probe, positions, counts, measured)
        prev_object, prev_probe = (cur_object, cur_probe)
        cur_object = ahead_object - object_rate * object_grad
        cur_probe = ahead_probe - probe_step * probe_grad
    return (cur_object, cur_probe)
```

```python
import jax
import jax.numpy as jnp
import ml_dtypes
import numpy as np
from jax import lax
from jax.experimental import pallas as pl
from jax.experimental.pallas import tpu as pltpu
from jax.sharding import PartitionSpec as P

ITERS = 2


momentum = 0.5
object_rate = 0.1
probe_rate = 0.25


def dft_tables(size):
    steps = np.arange(size)
    angle = (steps[:, None] * steps[None, :] % size) * (2.0 * np.pi / size)
    cosine, sine = np.cos(angle) / np.sqrt(size), np.sin(angle) / np.sqrt(size)
    ahead = np.block([[cosine, -sine], [sine, cosine]]).astype(np.float32)
    halves = []
    for table in (ahead, ahead.T):
        high = table.astype(ml_dtypes.bfloat16)
        low = (table - high.astype(np.float32)).astype(ml_dtypes.bfloat16)
        halves += [high, low]
    return halves


def split(values):
    high = values.astype(jnp.bfloat16)
    return high, (values - high.astype(jnp.float32)).astype(jnp.bfloat16)


def matmul(left, right):
    return jnp.dot(left, right, preferred_element_type=jnp.float32)


def from_right(values, high, low):
    values_high, values_low = split(values)
    return matmul(values_high, high) + (matmul(values_low, high) + matmul(values_high, low))


def from_left(high, low, values):
    values_high, values_low = split(values)
    return matmul(high, values_high) + (matmul(low, values_high) + matmul(high, values_low))


def gradient_kernel(
    scalars, mine, theirs, measured, ahead_high, ahead_low, behind_high, behind_low, keep, send,
    state, grad, *, group
):
    size = measured.shape[-1]
    slots = measured.shape[0]
    tiles = mine.shape[0] // size - 2
    me = scalars[0]
    live_slots = scalars[1]
    state[me] = mine[...]
    state[1 - me] = theirs[...]
    grad[...] = jnp.zeros_like(grad)
    lane = lax.broadcasted_iota(jnp.int32, (size, size), 1)
    base = tiles * size

    def plane(mode, part):
        return state[mode, base + part * size : base + (part + 1) * size, :]

    def rows_of(row, tile):
        return pl.ds(tile * (2 * size) + row, size)

    def one_group(first):
        places, patches, waves = [], [], []
        for index in range(group):
            slot = 2 * (first + index) + me
            row = scalars[2 + 2 * slot]
            col = scalars[3 + 2 * slot]
            tile = col // size
            shift = col % size
            places.append((slot, row, tile, shift))
            patch = []
            for part in range(2):
                near = state[part, rows_of(row, tile), :]
                far = state[part, rows_of(row, tile + 1), :]
                patch.append(
                    pltpu.roll(jnp.where(lane >= shift, near, far), (size - shift) % size, 1)
                )
            patches.append(patch)
            for mode in range(2):
                real, imag = plane(mode, 0), plane(mode, 1)
                waves.append(
                    jnp.concatenate(
                        [real * patch[0] - imag * patch[1], real * patch[1] + imag * patch[0]],
                        axis=1,
                    )
                )
        half = from_right(jnp.concatenate(waves, axis=0), ahead_high[...], ahead_low[...])
        scaled = []
        for index in range(group):
            first_mode = half[2 * index * size : (2 * index + 1) * size]
            second_mode = half[(2 * index + 1) * size : (2 * index + 2) * size]
            turned = jnp.concatenate(
                [
                    jnp.concatenate([first_mode[:, :size], second_mode[:, :size]], axis=1),
                    jnp.concatenate([first_mode[:, size:], second_mode[:, size:]], axis=1),
                ],
                axis=0,
            )
            far_field = from_left(behind_high[...], behind_low[...], turned)
            power = far_field * far_field
            power = power[:size] + power[size:]
            power = power[:, :size] + power[:, size:]
            slot = places[index][0]
            live = jnp.where(slot < live_slots, 1.0, 0.0).astype(jnp.float32)
            weight = (
                1.0 - jnp.sqrt(measured[first + index, 0]) * lax.rsqrt(power + 1.0)
            ) * live
            weight = jnp.concatenate([weight, weight], axis=1)
            weight = jnp.concatenate([weight, weight], axis=0)
            back = from_left(ahead_high[...], ahead_low[...], weight * far_field)
            for mode in range(2):
                lanes = slice(mode * size, (mode + 1) * size)
                scaled.append(jnp.concatenate([back[:size, lanes], back[size:, lanes]], axis=1))
        chi = from_right(jnp.concatenate(scaled, axis=0), behind_high[...], behind_low[...])
        for index in range(group):
            _, row, tile, shift = places[index]
            pieces = [0.0, 0.0]
            for mode in range(2):
                start = (2 * index + mode) * size
                chi_real = chi[start : start + size, :size]
                chi_imag = chi[start : start + size, size:]
                real, imag = plane(mode, 0), plane(mode, 1)
                pieces[0] = pieces[0] + (real * chi_real + imag * chi_imag)
                pieces[1] = pieces[1] + (real * chi_imag - imag * chi_real)
                patch_real, patch_imag = patches[index]
                grad[mode, base : base + size, :] += (
                    patch_real * chi_real + patch_imag * chi_imag
                )
                grad[mode, base + size : base + 2 * size, :] += (
                    patch_real * chi_imag - patch_imag * chi_real
                )
            for part in range(2):
                turned_back = pltpu.roll(pieces[part], shift, 1)
                inside = lane >= shift
                grad[part, rows_of(row, tile), :] += jnp.where(inside, turned_back, 0.0)
                grad[part, rows_of(row, tile + 1), :] += jnp.where(inside, 0.0, turned_back)

    @pl.loop(0, slots // group)
    def _(step):
        one_group(step * group)

    keep[...] = grad[me]
    send[...] = grad[1 - me]


def gradients(scalars, mine, theirs, measured):
    size = measured.shape[-1]
    slots = measured.shape[0] // 2
    shape = jax.ShapeDtypeStruct(mine.shape, jnp.float32)
    whole = pl.BlockSpec(mine.shape, lambda i, s: (0, 0))
    table = pl.BlockSpec((2 * size, 2 * size), lambda i, s: (0, 0))
    group = 4 if slots % 4 == 0 else 1

    def body(*refs):
        gradient_kernel(*refs, group=group)

    return pl.pallas_call(
        body,
        out_shape=(shape, shape),
        grid_spec=pltpu.PrefetchScalarGridSpec(
            num_scalar_prefetch=1,
            grid=(1,),
            in_specs=[
                whole,
                whole,
                pl.BlockSpec((slots, 1, size, size), lambda i, s: (0, s[0], 0, 0)),
                table,
                table,
                table,
                table,
            ],
            out_specs=[whole, whole],
            scratch_shapes=[
                pltpu.VMEM((2,) + mine.shape, jnp.float32),
                pltpu.VMEM((2,) + mine.shape, jnp.float32),
            ],
        ),
        compiler_params=pltpu.CompilerParams(vmem_limit_bytes=32 * 1024 * 1024),
        name="gradients",
    )(
        scalars,
        mine,
        theirs,
        measured.reshape(slots, 2, size, size),
        *[jnp.asarray(t) for t in dft_tables(size)],
    )


def neighbour_pairs(count, parity):
    pairs = [(i, i + 1) for i in range(parity, count - 1, 2)]
    return pairs + [(b, a) for a, b in pairs]


def sum_pairs(count, step):
    return [(i, i ^ (2 ** (step + 1) - 1)) for i in range(count)]


def swap_modes(block):
    return lax.ppermute(block, "mode", [(0, 1), (1, 0)])


def along_axis(block, axis, sides):
    count = lax.axis_size(axis)
    me = lax.axis_index(axis)
    low, high = sides
    steps = max(count - 1, 0).bit_length()
    done = 0
    for parity in (0, 1):
        pairs = neighbour_pairs(count, parity)
        if not pairs:
            continue
        is_low = me % 2 == parity
        shared = jnp.where(is_low, block[jnp.array(high)], block[jnp.array(low)])
        with_probe = parity == 0 or count == 4
        if with_probe:
            got = lax.ppermute(
                jnp.concatenate([shared, block[-2:]]), axis, sum_pairs(count, done)
            )
            done += 1
            probe = block[-2:] + got[-2:]
            got = got[:-2]
        else:
            got = lax.ppermute(shared, axis, pairs)
            probe = block[-2:]
        to_high = jnp.where(is_low & (me < count - 1), got, 0.0)
        to_low = jnp.where(jnp.logical_not(is_low) & (me > 0), got, 0.0)
        parts = [block[i] for i in range(block.shape[0] - 2)]
        for place, (a, b) in enumerate(zip(low, high, strict=True)):
            parts[a] = parts[a] + to_low[place]
            parts[b] = parts[b] + to_high[place]
        block = jnp.concatenate([jnp.stack(parts), probe])
    while done < steps:
        probe = block[-2:]
        probe = probe + lax.ppermute(probe, axis, sum_pairs(count, done))
        block = jnp.concatenate([block[:-2], probe])
        done += 1
    return block


def combine(keep, send, size):
    block = (keep + swap_modes(send)).reshape(-1, size, size)
    columns = (block.shape[0] - 2) // 2
    block = along_axis(block, "col", ((0, 1), (2 * columns - 2, 2 * columns - 1)))
    uppers = tuple(2 * i for i in range(columns))
    lowers = tuple(2 * i + 1 for i in range(columns))
    return along_axis(block, "row", (uppers, lowers))


def padded(block, sides, width):
    for axis, dim in sides:
        count = lax.axis_size(axis)
        me = lax.axis_index(axis)
        first = lax.slice_in_dim(block, 0, width, axis=dim)
        last = lax.slice_in_dim(block, block.shape[dim] - width, None, axis=dim)
        low = high = jnp.zeros_like(first)
        for parity in (0, 1):
            pairs = neighbour_pairs(count, parity)
            if not pairs:
                continue
            is_low = me % 2 == parity
            got = lax.ppermute(jnp.where(is_low, last, first), axis, pairs)
            low = jnp.where(is_low, low, got)
            high = jnp.where(is_low, got, high)
        block = jnp.concatenate([low, block, high], axis=dim)
    return block


def on_device(obj, probe, positions, counts, measured):
    size = probe.shape[-1]
    half = size // 2
    tile_rows, tile_cols = obj.shape[1:]
    slot_count = positions.shape[2]
    me = lax.axis_index("mode")
    row = lax.axis_index("row")
    col = lax.axis_index("col")
    corner = jnp.stack([row * tile_rows - half, col * tile_cols - half])
    offsets = positions[0, 0] - corner[None, :]
    scalars = jnp.concatenate([jnp.stack([me, counts[0, 0]]), offsets.reshape(-1)])
    probe_step = probe_rate / (slot_count * lax.axis_size("row") * lax.axis_size("col"))

    own = lax.dynamic_index_in_dim(obj, me, 0, keepdims=False)
    extended = padded(own, (("col", 1), ("row", 0)), half)
    ext_rows, ext_cols = extended.shape
    columns = ext_cols // size
    blocks = extended.reshape(2, size, columns, size).transpose(2, 0, 1, 3)
    start = jnp.concatenate([blocks.reshape(2 * columns, size, size), probe[0]])

    global_rows = (
        jnp.arange(ext_rows, dtype=jnp.int32).reshape(1, 2, size, 1) + row * tile_rows - half
    )
    global_cols = (
        jnp.arange(ext_cols, dtype=jnp.int32).reshape(columns, 1, 1, size) + col * tile_cols - half
    )
    inside = (
        (global_rows >= 0)
        & (global_rows < tile_rows * lax.axis_size("row"))
        & (global_cols >= 0)
        & (global_cols < tile_cols * lax.axis_size("col"))
    )
    rates = jnp.concatenate(
        [
            jnp.where(inside, object_rate, 0.0).reshape(2 * columns, size, size),
            jnp.full((2, size, size), probe_step, jnp.float32),
        ]
    ).astype(jnp.float32)

    previous, current = start, start
    for iteration in range(ITERS):
        ahead = current + momentum * (current - previous)
        flat = ahead.reshape(-1, size)
        keep, send = gradients(scalars, flat, swap_modes(flat), measured[0, 0])
        total = combine(keep, send, size)
        previous, current = current, ahead - rates * total

    tile = current[:-2].reshape(columns, 2, size, size).transpose(1, 2, 0, 3)
    tile = tile.reshape(ext_rows, ext_cols)[half : half + tile_rows, half : half + tile_cols]
    other = swap_modes(tile)
    whole = jnp.stack([jnp.where(me == 0, tile, other), jnp.where(me == 0, other, tile)])
    return (whole, current[None, -2:])


def solution(mesh):
    in_specs = (
        P(None, ("parts", "row"), "col"),
        P("mode", None, "parts", None),
        P("row", "col", "parts", None),
        P(("parts", "row"), "col"),
        P("row", "col", "parts", None, None),
    )
    out_specs = (P(None, ("parts", "row"), "col"), P("mode", None, "parts", None))
    return jax.shard_map(
        on_device, mesh=mesh, in_specs=in_specs, out_specs=out_specs, check_vma=False
    )
```

```python
import jax
import jax.numpy as jnp
import ml_dtypes
import numpy as np
from jax import lax
from jax.experimental import pallas as pl
from jax.experimental.pallas import tpu as pltpu
from jax.sharding import PartitionSpec as P

ITERS = 2


momentum = 0.5
object_rate = 0.1
probe_rate = 0.25


def dft_tables(size):
    steps = np.arange(size)
    angle = (steps[:, None] * steps[None, :] % size) * (2.0 * np.pi / size)
    cosine, sine = np.cos(angle) / np.sqrt(size), np.sin(angle) / np.sqrt(size)
    ahead = np.block([[cosine, -sine], [sine, cosine]]).astype(np.float32)
    halves = []
    for table in (ahead, ahead.T):
        high = table.astype(ml_dtypes.bfloat16)
        low = (table - high.astype(np.float32)).astype(ml_dtypes.bfloat16)
        halves += [high, low]
    return halves


def split(values):
    high = values.astype(jnp.bfloat16)
    return high, (values - high.astype(jnp.float32)).astype(jnp.bfloat16)


def matmul(left, right):
    return jnp.dot(left, right, preferred_element_type=jnp.float32)


def from_right(values, high, low):
    values_high, values_low = split(values)
    return matmul(values_high, high) + (matmul(values_low, high) + matmul(values_high, low))


def from_left(high, low, values):
    values_high, values_low = split(values)
    return matmul(high, values_high) + (matmul(low, values_high) + matmul(high, values_low))


def gradient_kernel(scalars, *refs, columns, group):
    mine, theirs = refs[: columns + 1], refs[columns + 1 : 2 * columns + 2]
    measured, ahead_high, ahead_low, behind_high, behind_low = refs[2 * columns + 2 :][:5]
    keep, send, state, grad = refs[2 * columns + 7 :]
    size = measured.shape[-1]
    slots = measured.shape[0]
    me = scalars[0]
    live_slots = scalars[1]
    half_mine = scalars[2]
    lane = lax.broadcasted_iota(jnp.int32, (size, size), 1)
    base = columns * 2 * size

    def region(tile, half):
        return pl.ds(pl.multiple_of(tile * 2 * size + half * size, size), size)

    for blocks, half, mode in ((mine, half_mine, me), (theirs, 1 - half_mine, 1 - me)):
        for part in range(2):
            rows = slice(part * size, (part + 1) * size)
            for tile in range(columns):
                state[part, region(tile, half), :] = blocks[tile][rows, :]
            state[mode, base + part * size : base + (part + 1) * size, :] = blocks[-1][rows, :]
    grad[...] = jnp.zeros_like(grad)

    def plane(mode, part):
        return state[mode, base + part * size : base + (part + 1) * size, :]

    def rows_of(row, tile):
        return pl.ds(tile * (2 * size) + row, size)

    def one_group(first):
        places, patches, waves = [], [], []
        for index in range(group):
            slot = 2 * (first + index) + me
            row = scalars[3 + 2 * slot]
            col = scalars[4 + 2 * slot]
            tile = col // size
            shift = col % size
            places.append((slot, row, tile, shift))
            patch = []
            for part in range(2):
                near = state[part, rows_of(row, tile), :]
                far = state[part, rows_of(row, tile + 1), :]
                patch.append(
                    pltpu.roll(jnp.where(lane >= shift, near, far), (size - shift) % size, 1)
                )
            patches.append(patch)
            for mode in range(2):
                real, imag = plane(mode, 0), plane(mode, 1)
                waves.append(
                    jnp.concatenate(
                        [real * patch[0] - imag * patch[1], real * patch[1] + imag * patch[0]],
                        axis=1,
                    )
                )
        half = from_right(jnp.concatenate(waves, axis=0), ahead_high[...], ahead_low[...])
        scaled = []
        for index in range(group):
            first_mode = half[2 * index * size : (2 * index + 1) * size]
            second_mode = half[(2 * index + 1) * size : (2 * index + 2) * size]
            turned = jnp.concatenate(
                [
                    jnp.concatenate([first_mode[:, :size], second_mode[:, :size]], axis=1),
                    jnp.concatenate([first_mode[:, size:], second_mode[:, size:]], axis=1),
                ],
                axis=0,
            )
            far_field = from_left(behind_high[...], behind_low[...], turned)
            power = far_field * far_field
            power = power[:size] + power[size:]
            power = power[:, :size] + power[:, size:]
            slot = places[index][0]
            live = jnp.where(slot < live_slots, 1.0, 0.0).astype(jnp.float32)
            weight = (
                1.0 - jnp.sqrt(measured[first + index, 0]) * lax.rsqrt(power + 1.0)
            ) * live
            weight = jnp.concatenate([weight, weight], axis=1)
            weight = jnp.concatenate([weight, weight], axis=0)
            back = from_left(ahead_high[...], ahead_low[...], weight * far_field)
            for mode in range(2):
                lanes = slice(mode * size, (mode + 1) * size)
                scaled.append(jnp.concatenate([back[:size, lanes], back[size:, lanes]], axis=1))
        chi = from_right(jnp.concatenate(scaled, axis=0), behind_high[...], behind_low[...])
        for index in range(group):
            _, row, tile, shift = places[index]
            pieces = [0.0, 0.0]
            for mode in range(2):
                start = (2 * index + mode) * size
                chi_real = chi[start : start + size, :size]
                chi_imag = chi[start : start + size, size:]
                real, imag = plane(mode, 0), plane(mode, 1)
                pieces[0] = pieces[0] + (real * chi_real + imag * chi_imag)
                pieces[1] = pieces[1] + (real * chi_imag - imag * chi_real)
                patch_real, patch_imag = patches[index]
                grad[mode, base : base + size, :] += (
                    patch_real * chi_real + patch_imag * chi_imag
                )
                grad[mode, base + size : base + 2 * size, :] += (
                    patch_real * chi_imag - patch_imag * chi_real
                )
            for part in range(2):
                turned_back = pltpu.roll(pieces[part], shift, 1)
                inside = lane >= shift
                grad[part, rows_of(row, tile), :] += jnp.where(inside, turned_back, 0.0)
                grad[part, rows_of(row, tile + 1), :] += jnp.where(inside, 0.0, turned_back)

    @pl.loop(0, slots // group)
    def _(step):
        one_group(step * group)

    for target, half, mode in ((keep, half_mine, me), (send, 1 - half_mine, 1 - me)):
        for part in range(2):
            for tile in range(columns):
                start = (2 * tile + part) * size
                target[start : start + size, :] = grad[part, region(tile, half), :]
            start = base + part * size
            target[start : start + size, :] = grad[mode, start : start + size, :]


def gradients(scalars, mine, theirs, measured):
    size = measured.shape[-1]
    slots = measured.shape[0] // 2
    columns = len(mine) - 1
    height = (columns + 1) * 2 * size
    shape = jax.ShapeDtypeStruct((height, size), jnp.float32)
    whole = pl.BlockSpec((height, size), lambda i, s: (0, 0))
    block = pl.BlockSpec((2 * size, size), lambda i, s: (0, 0))
    table = pl.BlockSpec((2 * size, 2 * size), lambda i, s: (0, 0))
    group = 4 if slots % 4 == 0 else 1

    def body(*refs):
        gradient_kernel(*refs, columns=columns, group=group)

    return pl.pallas_call(
        body,
        out_shape=(shape, shape),
        grid_spec=pltpu.PrefetchScalarGridSpec(
            num_scalar_prefetch=1,
            grid=(1,),
            in_specs=[block] * (2 * columns + 2)
            + [pl.BlockSpec((slots, 1, size, size), lambda i, s: (0, s[0], 0, 0))]
            + [table] * 4,
            out_specs=[whole, whole],
            scratch_shapes=[
                pltpu.VMEM((2, height, size), jnp.float32),
                pltpu.VMEM((2, height, size), jnp.float32),
            ],
        ),
        compiler_params=pltpu.CompilerParams(vmem_limit_bytes=24 * 1024 * 1024),
        name="gradients",
    )(
        scalars,
        *mine,
        *theirs,
        measured.reshape(slots, 2, size, size),
        *[jnp.asarray(t) for t in dft_tables(size)],
    )


def swap_modes(block):
    return lax.ppermute(block, "mode", [(0, 1), (1, 0)])


def swap_rows(block):
    count = lax.axis_size("row")
    route = []
    for row in range(count):
        for mode in range(2):
            other = row + 1 if row % 2 == mode else row - 1
            other = other if 0 <= other < count else row
            route.append((2 * row + mode, 2 * other + mode))
    return lax.ppermute(block, ("row", "mode"), route)


def swap_cols(to_low, to_high):
    count = lax.axis_size("col")
    col = lax.axis_index("col")
    from_low = from_high = jnp.zeros_like(to_low)
    for parity in range(min(2, count - 1)):
        route = []
        for i in range(count):
            other = i + 1 if i % 2 == parity else i - 1
            route.append((i, other if 0 <= other < count else i))
        is_low = col % 2 == parity
        got = lax.ppermute(jnp.where(is_low, to_high, to_low), "col", route)
        from_high = jnp.where(is_low & (col < count - 1), got, from_high)
        from_low = jnp.where(jnp.logical_not(is_low) & (col > 0), got, from_low)
    return from_low, from_high


def sum_tiles(block):
    for axis in ("col", "row"):
        count = lax.axis_size(axis)
        reach = 1
        while reach < count:
            block = block + lax.ppermute(block, axis, [(i, i ^ (2 * reach - 1)) for i in range(count)])
            reach *= 2
    return block


def on_device(obj, probe, positions, counts, measured):
    size = probe.shape[-1]
    half = size // 2
    tile_rows, tile_cols = obj.shape[1:]
    columns = tile_cols // size + 1
    slot_count = positions.shape[2]
    rows_count, cols_count = lax.axis_size("row"), lax.axis_size("col")
    me = lax.axis_index("mode")
    row = lax.axis_index("row")
    col = lax.axis_index("col")
    lower = row % 2 == me
    paired = jnp.where(lower, row < rows_count - 1, row > 0)
    half_mine = lower.astype(jnp.int32)
    corner = jnp.stack([row * tile_rows - half, col * tile_cols - half])
    offsets = positions[0, 0] - corner[None, :]
    scalars = jnp.concatenate([jnp.stack([me, counts[0, 0], half_mine]), offsets.reshape(-1)])
    probe_step = probe_rate / (slot_count * rows_count * cols_count)

    strip = jnp.where(lower, obj[:, half:], obj[:, :half])
    beside = jnp.where(paired, swap_rows(strip), 0.0)
    region = jnp.concatenate(
        [jnp.where(lower, strip, beside), jnp.where(lower, beside, strip)], axis=1
    )
    from_low, from_high = swap_cols(region[:, :, :half], region[:, :, tile_cols - half :])
    wide = jnp.concatenate([from_low, region, from_high], axis=2)
    start = [
        wide[:, :, tile * size : (tile + 1) * size].reshape(2 * size, size)
        for tile in range(columns)
    ] + [probe[0].reshape(2 * size, size)]

    ext_rows = jnp.arange(size, dtype=jnp.int32)[:, None] + half_mine * size - half
    ext_rows = jnp.concatenate([ext_rows, ext_rows]) + row * tile_rows
    rows_inside = (ext_rows >= 0) & (ext_rows < tile_rows * rows_count)
    rates = []
    for tile in range(columns):
        ext_cols = jnp.arange(size, dtype=jnp.int32)[None, :] + tile * size - half + col * tile_cols
        inside = rows_inside & (ext_cols >= 0) & (ext_cols < tile_cols * cols_count)
        rates.append(jnp.where(inside, jnp.float32(object_rate), 0.0))

    previous, current = start, start
    for iteration in range(ITERS):
        ahead = [x + momentum * (x - y) for x, y in zip(current, previous, strict=True)]
        keep, send = gradients(scalars, ahead, [swap_modes(x) for x in ahead], measured[0, 0])
        total = keep + swap_modes(send)
        previous = current
        probe_grad = sum_tiles(total[columns * 2 * size :])
        object_grad = total[: columns * 2 * size]
        new_probe = ahead[-1] - probe_step * probe_grad
        if iteration < ITERS - 1:
            object_grad = object_grad + jnp.where(paired, swap_rows(object_grad), 0.0)
            parts = [
                object_grad[tile * 2 * size : (tile + 1) * 2 * size] for tile in range(columns)
            ]
            from_low, from_high = swap_cols(parts[0], parts[-1])
            parts[0] = parts[0] + from_low
            parts[-1] = parts[-1] + from_high
            current = [
                x - rate * g for x, rate, g in zip(ahead, rates, parts, strict=False)
            ] + [new_probe]
        else:
            object_grad = object_grad.reshape(columns, 2, size, size)
            given = jnp.where(lower, object_grad[:, :, half:], object_grad[:, :, :half])
            owned = jnp.where(lower, object_grad[:, :, :half], object_grad[:, :, half:])
            owned = owned + jnp.where(paired, swap_rows(given), 0.0)
            from_low, from_high = swap_cols(owned[0, :, :, :half], owned[-1, :, :, half:])
            owned = jnp.concatenate(
                [owned[0, :, :, half:] + from_low]
                + [owned[tile] for tile in range(1, columns - 1)]
                + [owned[-1, :, :, :half] + from_high],
                axis=2,
            )
            held = jnp.concatenate([x.reshape(2, size, size) for x in ahead[:-1]], axis=2)
            held = jnp.where(lower, held[:, :half], held[:, half:])
            strip = held[:, :, half : half + tile_cols] - object_rate * owned

    other = swap_modes(strip)
    whole = jnp.concatenate(
        [jnp.where(lower, other, strip), jnp.where(lower, strip, other)], axis=1
    )
    return (whole, new_probe.reshape(1, 2, size, size))


def solution(mesh):
    in_specs = (
        P(None, ("parts", "row"), "col"),
        P("mode", None, "parts", None),
        P("row", "col", "parts", None),
        P(("parts", "row"), "col"),
        P("row", "col", "parts", None, None),
    )
    out_specs = (P(None, ("parts", "row"), "col"), P("mode", None, "parts", None))
    return jax.shard_map(
        on_device, mesh=mesh, in_specs=in_specs, out_specs=out_specs, check_vma=False
    )
```

```python
import jax
import jax.numpy as jnp
import ml_dtypes
import numpy as np
from jax import lax
from jax.experimental import pallas as pl
from jax.experimental.pallas import tpu as pltpu
from jax.sharding import PartitionSpec as P

ITERS = 2


momentum = 0.5
object_rate = 0.1
probe_rate = 0.25


def dft_tables(size):
    steps = np.arange(size)
    angle = (steps[:, None] * steps[None, :] % size) * (2.0 * np.pi / size)
    cosine, sine = np.cos(angle) / np.sqrt(size), np.sin(angle) / np.sqrt(size)
    ahead = np.block([[cosine, -sine], [sine, cosine]]).astype(np.float32)
    halves = []
    for table in (ahead, ahead.T):
        high = table.astype(ml_dtypes.bfloat16)
        low = (table - high.astype(np.float32)).astype(ml_dtypes.bfloat16)
        halves += [high, low]
    return halves


def split(values):
    high = values.astype(jnp.bfloat16)
    return high, (values - high.astype(jnp.float32)).astype(jnp.bfloat16)


def matmul(left, right):
    return jnp.dot(left, right, preferred_element_type=jnp.float32)


def from_right(values, high, low):
    values_high, values_low = split(values)
    return matmul(values_high, high) + (matmul(values_low, high) + matmul(values_high, low))


def from_left(high, low, values):
    values_high, values_low = split(values)
    return matmul(high, values_high) + (matmul(low, values_high) + matmul(high, values_low))


def gradient_kernel(scalars, *refs, columns, group):
    mine, theirs = refs[: columns + 1], refs[columns + 1 : 2 * columns + 2]
    measured, ahead_high, ahead_low, behind_high, behind_low = refs[2 * columns + 2 :][:5]
    keep, send, state, grad = refs[2 * columns + 7 :]
    size = measured.shape[-1]
    slots = measured.shape[0]
    me = scalars[0]
    live_slots = scalars[1]
    half_mine = scalars[2]
    lane = lax.broadcasted_iota(jnp.int32, (size, size), 1)
    base = columns * 2 * size

    def region(tile, half):
        return pl.ds(pl.multiple_of(tile * 2 * size + half * size, size), size)

    for blocks, half, mode in ((mine, half_mine, me), (theirs, 1 - half_mine, 1 - me)):
        for part in range(2):
            rows = slice(part * size, (part + 1) * size)
            for tile in range(columns):
                state[part, region(tile, half), :] = blocks[tile][rows, :]
            state[mode, base + part * size : base + (part + 1) * size, :] = blocks[-1][rows, :]
    grad[...] = jnp.zeros_like(grad)

    def plane(mode, part):
        return state[mode, base + part * size : base + (part + 1) * size, :]

    def rows_of(row, tile):
        return pl.ds(tile * (2 * size) + row, size)

    def one_group(first):
        places, patches, waves = [], [], []
        for index in range(group):
            slot = 2 * (first + index) + me
            row = scalars[3 + 2 * slot]
            col = scalars[4 + 2 * slot]
            tile = col // size
            shift = col % size
            places.append((slot, row, tile, shift))
            patch = []
            for part in range(2):
                near = state[part, rows_of(row, tile), :]
                far = state[part, rows_of(row, tile + 1), :]
                patch.append(
                    pltpu.roll(jnp.where(lane >= shift, near, far), (size - shift) % size, 1)
                )
            patches.append(patch)
            for mode in range(2):
                real, imag = plane(mode, 0), plane(mode, 1)
                waves.append(
                    jnp.concatenate(
                        [real * patch[0] - imag * patch[1], real * patch[1] + imag * patch[0]],
                        axis=1,
                    )
                )
        half = from_right(jnp.concatenate(waves, axis=0), ahead_high[...], ahead_low[...])
        scaled = []
        for index in range(group):
            first_mode = half[2 * index * size : (2 * index + 1) * size]
            second_mode = half[(2 * index + 1) * size : (2 * index + 2) * size]
            turned = jnp.concatenate(
                [
                    jnp.concatenate([first_mode[:, :size], second_mode[:, :size]], axis=1),
                    jnp.concatenate([first_mode[:, size:], second_mode[:, size:]], axis=1),
                ],
                axis=0,
            )
            far_field = from_left(behind_high[...], behind_low[...], turned)
            power = far_field * far_field
            power = power[:size] + power[size:]
            power = power[:, :size] + power[:, size:]
            slot = places[index][0]
            live = jnp.where(slot < live_slots, 1.0, 0.0).astype(jnp.float32)
            weight = (
                1.0 - jnp.sqrt(measured[first + index, 0]) * lax.rsqrt(power + 1.0)
            ) * live
            weight = jnp.concatenate([weight, weight], axis=1)
            weight = jnp.concatenate([weight, weight], axis=0)
            back = from_left(ahead_high[...], ahead_low[...], weight * far_field)
            for mode in range(2):
                lanes = slice(mode * size, (mode + 1) * size)
                scaled.append(jnp.concatenate([back[:size, lanes], back[size:, lanes]], axis=1))
        chi = from_right(jnp.concatenate(scaled, axis=0), behind_high[...], behind_low[...])
        for index in range(group):
            _, row, tile, shift = places[index]
            pieces = [0.0, 0.0]
            for mode in range(2):
                start = (2 * index + mode) * size
                chi_real = chi[start : start + size, :size]
                chi_imag = chi[start : start + size, size:]
                real, imag = plane(mode, 0), plane(mode, 1)
                pieces[0] = pieces[0] + (real * chi_real + imag * chi_imag)
                pieces[1] = pieces[1] + (real * chi_imag - imag * chi_real)
                patch_real, patch_imag = patches[index]
                grad[mode, base : base + size, :] += (
                    patch_real * chi_real + patch_imag * chi_imag
                )
                grad[mode, base + size : base + 2 * size, :] += (
                    patch_real * chi_imag - patch_imag * chi_real
                )
            for part in range(2):
                turned_back = pltpu.roll(pieces[part], shift, 1)
                inside = lane >= shift
                grad[part, rows_of(row, tile), :] += jnp.where(inside, turned_back, 0.0)
                grad[part, rows_of(row, tile + 1), :] += jnp.where(inside, 0.0, turned_back)

    @pl.loop(0, slots // group)
    def _(step):
        one_group(step * group)

    for target, half, mode in ((keep, half_mine, me), (send, 1 - half_mine, 1 - me)):
        for part in range(2):
            for tile in range(columns):
                start = (2 * tile + part) * size
                target[start : start + size, :] = grad[part, region(tile, half), :]
            start = base + part * size
            target[start : start + size, :] = grad[mode, start : start + size, :]


def gradients(scalars, mine, theirs, measured):
    size = measured.shape[-1]
    slots = measured.shape[0] // 2
    columns = len(mine) - 1
    height = (columns + 1) * 2 * size
    shape = jax.ShapeDtypeStruct((height, size), jnp.float32)
    whole = pl.BlockSpec((height, size), lambda i, s: (0, 0))
    block = pl.BlockSpec((2 * size, size), lambda i, s: (0, 0))
    table = pl.BlockSpec((2 * size, 2 * size), lambda i, s: (0, 0))
    group = 4 if slots % 4 == 0 else 1

    def body(*refs):
        gradient_kernel(*refs, columns=columns, group=group)

    return pl.pallas_call(
        body,
        out_shape=(shape, shape),
        grid_spec=pltpu.PrefetchScalarGridSpec(
            num_scalar_prefetch=1,
            grid=(1,),
            in_specs=[block] * (2 * columns + 2)
            + [pl.BlockSpec((slots, 1, size, size), lambda i, s: (0, s[0], 0, 0))]
            + [table] * 4,
            out_specs=[whole, whole],
            scratch_shapes=[
                pltpu.VMEM((2, height, size), jnp.float32),
                pltpu.VMEM((2, height, size), jnp.float32),
            ],
        ),
        compiler_params=pltpu.CompilerParams(vmem_limit_bytes=24 * 1024 * 1024),
        name="gradients",
    )(
        scalars,
        *mine,
        *theirs,
        measured.reshape(slots, 2, size, size),
        *[jnp.asarray(t) for t in dft_tables(size)],
    )


def swap_modes(block):
    return lax.ppermute(block, "mode", [(0, 1), (1, 0)])


def paired_with(index, parity, count):
    other = index + 1 if index % 2 == parity else index - 1
    return other if 0 <= other < count else None


def swap_neighbours(block, col_parity=None):
    rows, cols = lax.axis_size("row"), lax.axis_size("col")
    route = []
    for row in range(rows):
        for col in range(cols):
            for mode in range(2):
                to_row = paired_with(row, mode, rows)
                to_col = col if col_parity is None else paired_with(col, col_parity, cols)
                if to_col is None:
                    to_row, to_col = row, col
                elif to_row is None:
                    to_row = row
                    to_col = col ^ 1 if cols % 2 == 0 and col_parity is None else to_col
                route.append(
                    ((row * cols + col) * 2 + mode, (to_row * cols + to_col) * 2 + mode)
                )
    return lax.ppermute(block, ("row", "col", "mode"), route)


def from_cols(blocks, send):
    count = lax.axis_size("col")
    col = lax.axis_index("col")
    to_low, to_high = blocks
    from_low = from_high = jnp.zeros_like(to_low)
    for parity in range(min(2, count - 1)):
        is_low = col % 2 == parity
        got = send(jnp.where(is_low, to_high, to_low), parity)
        from_high = jnp.where(is_low & (col < count - 1), got, from_high)
        from_low = jnp.where(jnp.logical_not(is_low) & (col > 0), got, from_low)
    return from_low, from_high


def swap_cols(block, parity):
    count = lax.axis_size("col")
    others = [paired_with(i, parity, count) for i in range(count)]
    return lax.ppermute(block, "col", [(i, i if o is None else o) for i, o in enumerate(others)])


def sum_tiles(block):
    rows, cols = lax.axis_size("row"), lax.axis_size("col")
    along_cols = [(0, 1 << k) for k in range((cols - 1).bit_length())]
    along_rows = [(1 << k, 0) for k in range((rows - 1).bit_length())]
    if len(along_rows) > 1:
        turned = [(3, 0)] + along_cols + along_rows[:1] + along_rows[2:]
    else:
        turned = along_rows + along_cols
    for steps in zip(along_cols + along_rows, turned, strict=True):
        route = []
        for row in range(rows):
            for col in range(cols):
                for mode in range(2):
                    to_row, to_col = row ^ steps[mode][0], col ^ steps[mode][1]
                    route.append(
                        ((row * cols + col) * 2 + mode, (to_row * cols + to_col) * 2 + mode)
                    )
        block = block + lax.ppermute(block, ("row", "col", "mode"), route)
    return block


def on_device(obj, probe, positions, counts, measured):
    size = probe.shape[-1]
    half = size // 2
    tile_rows, tile_cols = obj.shape[1:]
    columns = tile_cols // size + 1
    slot_count = positions.shape[2]
    rows_count, cols_count = lax.axis_size("row"), lax.axis_size("col")
    me = lax.axis_index("mode")
    row = lax.axis_index("row")
    col = lax.axis_index("col")
    lower = row % 2 == me
    paired = jnp.where(lower, row < rows_count - 1, row > 0)
    half_mine = lower.astype(jnp.int32)
    corner = jnp.stack([row * tile_rows - half, col * tile_cols - half])
    offsets = positions[0, 0] - corner[None, :]
    scalars = jnp.concatenate([jnp.stack([me, counts[0, 0], half_mine]), offsets.reshape(-1)])
    probe_step = probe_rate / (slot_count * rows_count * cols_count)

    strip = jnp.where(lower, obj[:, half:], obj[:, :half])
    edges = (strip[:, :, :half], strip[:, :, tile_cols - half :])
    beside = swap_neighbours(strip)
    strip_low, strip_high = from_cols(edges, swap_cols)
    corner_low, corner_high = from_cols(edges, swap_neighbours)
    strip = jnp.concatenate([strip_low, strip, strip_high], axis=2)
    beside = jnp.concatenate([corner_low, beside, corner_high], axis=2)
    beside = jnp.where(paired, beside, 0.0)
    wide = jnp.concatenate(
        [jnp.where(lower, strip, beside), jnp.where(lower, beside, strip)], axis=1
    )
    start = [
        wide[:, :, tile * size : (tile + 1) * size].reshape(2 * size, size)
        for tile in range(columns)
    ] + [probe[0].reshape(2 * size, size)]

    ext_rows = jnp.arange(size, dtype=jnp.int32)[:, None] + half_mine * size - half
    ext_rows = jnp.concatenate([ext_rows, ext_rows]) + row * tile_rows
    rows_inside = (ext_rows >= 0) & (ext_rows < tile_rows * rows_count)
    rates = []
    for tile in range(columns):
        ext_cols = jnp.arange(size, dtype=jnp.int32)[None, :] + tile * size - half + col * tile_cols
        inside = rows_inside & (ext_cols >= 0) & (ext_cols < tile_cols * cols_count)
        rates.append(jnp.where(inside, jnp.float32(object_rate), 0.0))

    previous, current = start, start
    for iteration in range(ITERS):
        ahead = [x + momentum * (x - y) for x, y in zip(current, previous, strict=True)]
        keep, send = gradients(scalars, ahead, [swap_modes(x) for x in ahead], measured[0, 0])
        total = keep + swap_modes(send)
        previous = current
        probe_grad = sum_tiles(total[columns * 2 * size :])
        object_grad = total[: columns * 2 * size]
        new_probe = ahead[-1] - probe_step * probe_grad
        if iteration < ITERS - 1:
            object_grad = object_grad + jnp.where(paired, swap_neighbours(object_grad), 0.0)
            parts = [
                object_grad[tile * 2 * size : (tile + 1) * 2 * size] for tile in range(columns)
            ]
            from_low, from_high = from_cols((parts[0], parts[-1]), swap_cols)
            parts[0] = parts[0] + from_low
            parts[-1] = parts[-1] + from_high
            current = [
                x - rate * g for x, rate, g in zip(ahead, rates, parts, strict=False)
            ] + [new_probe]
        else:
            object_grad = object_grad.reshape(columns, 2, size, size)
            given = jnp.where(lower, object_grad[:, :, half:], object_grad[:, :, :half])
            owned = jnp.where(lower, object_grad[:, :, :half], object_grad[:, :, half:])
            owned = owned + jnp.where(paired, swap_neighbours(given), 0.0)
            edges = (owned[0, :, :, :half], owned[-1, :, :, half:])
            from_low, from_high = from_cols(edges, swap_cols)
            owned = jnp.concatenate(
                [owned[0, :, :, half:] + from_low]
                + [owned[tile] for tile in range(1, columns - 1)]
                + [owned[-1, :, :, :half] + from_high],
                axis=2,
            )
            held = jnp.concatenate([x.reshape(2, size, size) for x in ahead[:-1]], axis=2)
            held = jnp.where(lower, held[:, :half], held[:, half:])
            strip = held[:, :, half : half + tile_cols] - object_rate * owned

    other = swap_modes(strip)
    whole = jnp.concatenate(
        [jnp.where(lower, other, strip), jnp.where(lower, strip, other)], axis=1
    )
    return (whole, new_probe.reshape(1, 2, size, size))


def solution(mesh):
    in_specs = (
        P(None, ("parts", "row"), "col"),
        P("mode", None, "parts", None),
        P("row", "col", "parts", None),
        P(("parts", "row"), "col"),
        P("row", "col", "parts", None, None),
    )
    out_specs = (P(None, ("parts", "row"), "col"), P("mode", None, "parts", None))
    return jax.shard_map(
        on_device, mesh=mesh, in_specs=in_specs, out_specs=out_specs, check_vma=False
    )
```

```python
import jax
import jax.numpy as jnp
import ml_dtypes
import numpy as np
from jax import lax
from jax.experimental import pallas as pl
from jax.experimental.pallas import tpu as pltpu
from jax.sharding import PartitionSpec as P

ITERS = 2


momentum = 0.5
object_rate = 0.1
probe_rate = 0.25

VMEM_LIMIT = 16 * 1024 * 1024


def dft_tables(size):
    steps = np.arange(size)
    angle = (steps[:, None] * steps[None, :] % size) * (2.0 * np.pi / size)
    cosine, sine = np.cos(angle) / np.sqrt(size), np.sin(angle) / np.sqrt(size)
    ahead = np.block([[cosine, -sine], [sine, cosine]]).astype(np.float32)
    halves = []
    for table in (ahead, ahead.T):
        high = table.astype(ml_dtypes.bfloat16)
        low = (table - high.astype(np.float32)).astype(ml_dtypes.bfloat16)
        halves += [high, low]
    return halves


def split(values):
    high = values.astype(jnp.bfloat16)
    return high, (values - high.astype(jnp.float32)).astype(jnp.bfloat16)


def matmul(left, right):
    return jnp.dot(left, right, preferred_element_type=jnp.float32)


def from_right(values, high, low):
    values_high, values_low = split(values)
    return matmul(values_high, high) + (matmul(values_low, high) + matmul(values_high, low))


def from_left(high, low, values):
    values_high, values_low = split(values)
    return matmul(high, values_high) + (matmul(low, values_high) + matmul(high, values_low))


def window_of(scalars, index, size):
    me, corner_row, corner_col = scalars[0][0], scalars[0][2], scalars[0][3]
    slot = 2 * index + me
    row = scalars[1][0, slot] - corner_row
    col = scalars[1][1, slot] - corner_col
    return slot, row, col // size, col % size


def region(tile, half, size):
    return pl.ds(pl.multiple_of(tile * 2 * size + half * size, size), size)


def rows_of(row, tile, size):
    return pl.ds(tile * 2 * size + row, size)


def wave_kernel(place, positions, counts, *refs, columns, group):
    scalars = (place, positions)
    mine, theirs = refs[: columns + 1], refs[columns + 1 : 2 * columns + 2]
    measured, ahead_high, ahead_low, behind_high, behind_low = refs[2 * columns + 2 :][:5]
    keep, send, pieces, state, modes, grad = refs[2 * columns + 7 :]
    size = measured.shape[-1]
    slots = measured.shape[0]
    me, half_mine = place[0], place[1]
    live_slots = counts[0, 0]
    lane = lax.broadcasted_iota(jnp.int32, (size, size), 1)

    for blocks, half, mode in ((mine, half_mine, me), (theirs, 1 - half_mine, 1 - me)):
        for part in range(2):
            rows = slice(part * size, (part + 1) * size)
            for tile in range(columns):
                state[part, region(tile, half, size), :] = blocks[tile][rows, :]
        modes[mode] = blocks[-1][...]
    grad[...] = jnp.zeros_like(grad)

    def plane(mode, part):
        return modes[mode, part * size : (part + 1) * size, :]

    def one_group(first):
        windows, patches, waves = [], [], []
        for index in range(group):
            slot, row, tile, shift = window_of(scalars, first + index, size)
            windows.append(slot)
            patch = []
            for part in range(2):
                near = state[part, rows_of(row, tile, size), :]
                far = state[part, rows_of(row, tile + 1, size), :]
                patch.append(
                    pltpu.roll(jnp.where(lane >= shift, near, far), (size - shift) % size, 1)
                )
            patches.append(patch)
            for mode in range(2):
                real, imag = plane(mode, 0), plane(mode, 1)
                waves.append(
                    jnp.concatenate(
                        [real * patch[0] - imag * patch[1], real * patch[1] + imag * patch[0]],
                        axis=1,
                    )
                )
        half = from_right(jnp.concatenate(waves, axis=0), ahead_high[...], ahead_low[...])
        scaled = []
        for index in range(group):
            first_mode = half[2 * index * size : (2 * index + 1) * size]
            second_mode = half[(2 * index + 1) * size : (2 * index + 2) * size]
            turned = jnp.concatenate(
                [
                    jnp.concatenate([first_mode[:, :size], second_mode[:, :size]], axis=1),
                    jnp.concatenate([first_mode[:, size:], second_mode[:, size:]], axis=1),
                ],
                axis=0,
            )
            far_field = from_left(behind_high[...], behind_low[...], turned)
            power = far_field * far_field
            power = power[:size] + power[size:]
            power = power[:, :size] + power[:, size:]
            live = jnp.where(windows[index] < live_slots, 1.0, 0.0).astype(jnp.float32)
            weight = (
                1.0 - jnp.sqrt(measured[first + index, 0]) * lax.rsqrt(power + 1.0)
            ) * live
            weight = jnp.concatenate([weight, weight], axis=1)
            weight = jnp.concatenate([weight, weight], axis=0)
            back = from_left(ahead_high[...], ahead_low[...], weight * far_field)
            for mode in range(2):
                lanes = slice(mode * size, (mode + 1) * size)
                scaled.append(jnp.concatenate([back[:size, lanes], back[size:, lanes]], axis=1))
        chi = from_right(jnp.concatenate(scaled, axis=0), behind_high[...], behind_low[...])
        for index in range(group):
            total = [0.0, 0.0]
            for mode in range(2):
                start = (2 * index + mode) * size
                chi_real = chi[start : start + size, :size]
                chi_imag = chi[start : start + size, size:]
                real, imag = plane(mode, 0), plane(mode, 1)
                total[0] = total[0] + (real * chi_real + imag * chi_imag)
                total[1] = total[1] + (real * chi_imag - imag * chi_real)
                patch_real, patch_imag = patches[index]
                grad[mode, :size, :] += patch_real * chi_real + patch_imag * chi_imag
                grad[mode, size:, :] += patch_real * chi_imag - patch_imag * chi_real
            for part in range(2):
                pieces[first + index, part] = total[part]

    @pl.loop(0, slots // group)
    def _(step):
        one_group(step * group)

    keep[...] = grad[me]
    send[...] = grad[1 - me]


def place_kernel(place, positions, pieces, keep, send, grad, *, columns):
    size = pieces.shape[-1]
    half_mine = place[1]
    lane = lax.broadcasted_iota(jnp.int32, (size, size), 1)
    grad[...] = jnp.zeros_like(grad)
    for index in range(pieces.shape[0]):
        _, row, tile, shift = window_of((place, positions), index, size)
        inside = lane >= shift
        for part in range(2):
            turned = pltpu.roll(pieces[index, part], shift, 1)
            grad[part, rows_of(row, tile, size), :] += jnp.where(inside, turned, 0.0)
            grad[part, rows_of(row, tile + 1, size), :] += jnp.where(inside, 0.0, turned)
    for target, half in ((keep, half_mine), (send, 1 - half_mine)):
        for tile in range(columns):
            for part in range(2):
                start = (2 * tile + part) * size
                target[start : start + size, :] = grad[part, region(tile, half, size), :]


def whole_block(shape):
    return pl.BlockSpec(shape, lambda i, *_: (0,) * len(shape))


def waves(scalars, mine, theirs, measured):
    size = measured.shape[-1]
    slots = measured.shape[0] // 2
    columns = len(mine) - 1
    group = 4 if slots % 4 == 0 else 1
    pair = (2 * size, size)
    pieces = (slots, 2, size, size)

    def body(*refs):
        wave_kernel(*refs, columns=columns, group=group)

    return pl.pallas_call(
        body,
        out_shape=[jax.ShapeDtypeStruct(s, jnp.float32) for s in (pair, pair, pieces)],
        grid_spec=pltpu.PrefetchScalarGridSpec(
            num_scalar_prefetch=3,
            grid=(1,),
            in_specs=[whole_block(pair)] * (2 * columns + 2)
            + [pl.BlockSpec((slots, 1, size, size), lambda i, s, *_: (0, s[0], 0, 0))]
            + [whole_block((2 * size, 2 * size))] * 4,
            out_specs=[whole_block(s) for s in (pair, pair, pieces)],
            scratch_shapes=[
                pltpu.VMEM((2, columns * 2 * size, size), jnp.float32),
                pltpu.VMEM((2,) + pair, jnp.float32),
                pltpu.VMEM((2,) + pair, jnp.float32),
            ],
        ),
        compiler_params=pltpu.CompilerParams(vmem_limit_bytes=VMEM_LIMIT),
        name="waves",
    )(
        *scalars,
        *mine,
        *theirs,
        measured.reshape(slots, 2, size, size),
        *[jnp.asarray(t) for t in dft_tables(size)],
    )


def placed(scalars, pieces, columns):
    size = pieces.shape[-1]
    shape = (columns * 2 * size, size)

    def body(*refs):
        place_kernel(*refs, columns=columns)

    return pl.pallas_call(
        body,
        out_shape=[jax.ShapeDtypeStruct(shape, jnp.float32)] * 2,
        grid_spec=pltpu.PrefetchScalarGridSpec(
            num_scalar_prefetch=2,
            grid=(1,),
            in_specs=[whole_block(pieces.shape)],
            out_specs=[whole_block(shape)] * 2,
            scratch_shapes=[pltpu.VMEM((2,) + shape, jnp.float32)],
        ),
        compiler_params=pltpu.CompilerParams(vmem_limit_bytes=VMEM_LIMIT),
        name="placed",
    )(*scalars[:2], pieces)


def swap_modes(block):
    return lax.ppermute(block, "mode", [(0, 1), (1, 0)])


def paired_with(index, parity, count):
    other = index + 1 if index % 2 == parity else index - 1
    return other if 0 <= other < count else None


def swap_neighbours(block, col_parity=None):
    rows, cols = lax.axis_size("row"), lax.axis_size("col")
    route = []
    for row in range(rows):
        for col in range(cols):
            for mode in range(2):
                to_row = paired_with(row, mode, rows)
                to_col = col if col_parity is None else paired_with(col, col_parity, cols)
                if to_col is None:
                    to_row, to_col = row, col
                elif to_row is None:
                    to_row = row
                    to_col = col ^ 1 if cols % 2 == 0 and col_parity is None else to_col
                route.append(
                    ((row * cols + col) * 2 + mode, (to_row * cols + to_col) * 2 + mode)
                )
    return lax.ppermute(block, ("row", "col", "mode"), route)


def from_cols(blocks, send):
    count = lax.axis_size("col")
    col = lax.axis_index("col")
    to_low, to_high = blocks
    from_low = from_high = jnp.zeros_like(to_low)
    for parity in range(min(2, count - 1)):
        is_low = col % 2 == parity
        got = send(jnp.where(is_low, to_high, to_low), parity)
        from_high = jnp.where(is_low & (col < count - 1), got, from_high)
        from_low = jnp.where(jnp.logical_not(is_low) & (col > 0), got, from_low)
    return from_low, from_high


def swap_cols(block, parity):
    count = lax.axis_size("col")
    others = [paired_with(i, parity, count) for i in range(count)]
    return lax.ppermute(block, "col", [(i, i if o is None else o) for i, o in enumerate(others)])


def sum_tiles(block):
    rows, cols = lax.axis_size("row"), lax.axis_size("col")
    along_cols = [(0, 1 << k) for k in range((cols - 1).bit_length())]
    along_rows = [(1 << k, 0) for k in range((rows - 1).bit_length())]
    if len(along_rows) > 1:
        turned = [(3, 0)] + along_cols + along_rows[:1] + along_rows[2:]
    else:
        turned = along_rows + along_cols
    for steps in zip(along_cols + along_rows, turned, strict=True):
        route = []
        for row in range(rows):
            for col in range(cols):
                for mode in range(2):
                    to_row, to_col = row ^ steps[mode][0], col ^ steps[mode][1]
                    route.append(
                        ((row * cols + col) * 2 + mode, (to_row * cols + to_col) * 2 + mode)
                    )
        block = block + lax.ppermute(block, ("row", "col", "mode"), route)
    return block


def on_device(obj, probe, positions, counts, measured):
    size = probe.shape[-1]
    half = size // 2
    tile_rows, tile_cols = obj.shape[1:]
    columns = tile_cols // size + 1
    slot_count = positions.shape[2]
    rows_count, cols_count = lax.axis_size("row"), lax.axis_size("col")
    me = lax.axis_index("mode")
    row = lax.axis_index("row")
    col = lax.axis_index("col")
    lower = row % 2 == me
    paired = jnp.where(lower, row < rows_count - 1, row > 0)
    half_mine = lower.astype(jnp.int32)
    place = jnp.stack(
        [me, half_mine, row * tile_rows - half, col * tile_cols - half]
    ).astype(jnp.int32)
    scalars = (place, positions[0, 0].T, counts)
    probe_step = probe_rate / (slot_count * rows_count * cols_count)

    strip = jnp.where(lower, obj[:, half:], obj[:, :half])
    edges = (strip[:, :, :half], strip[:, :, tile_cols - half :])
    beside = swap_neighbours(strip)
    strip_low, strip_high = from_cols(edges, swap_cols)
    corner_low, corner_high = from_cols(edges, swap_neighbours)
    strip = jnp.concatenate([strip_low, strip, strip_high], axis=2)
    beside = jnp.concatenate([corner_low, beside, corner_high], axis=2)
    beside = jnp.where(paired, beside, 0.0)
    wide = jnp.concatenate(
        [jnp.where(lower, strip, beside), jnp.where(lower, beside, strip)], axis=1
    )
    start = [
        wide[:, :, tile * size : (tile + 1) * size].reshape(2 * size, size)
        for tile in range(columns)
    ] + [probe[0].reshape(2 * size, size)]

    ext_rows = jnp.arange(size, dtype=jnp.int32)[:, None] + half_mine * size - half
    ext_rows = jnp.concatenate([ext_rows, ext_rows]) + row * tile_rows
    rows_inside = (ext_rows >= 0) & (ext_rows < tile_rows * rows_count)
    rates = []
    for tile in range(columns):
        ext_cols = jnp.arange(size, dtype=jnp.int32)[None, :] + tile * size - half + col * tile_cols
        inside = rows_inside & (ext_cols >= 0) & (ext_cols < tile_cols * cols_count)
        rates.append(jnp.where(inside, jnp.float32(object_rate), 0.0))

    previous, current = start, start
    for iteration in range(ITERS):
        ahead = [x + momentum * (x - y) for x, y in zip(current, previous, strict=True)]
        keep, send, pieces = waves(scalars, ahead, [swap_modes(x) for x in ahead], measured[0, 0])
        probe_grad = keep + swap_modes(send)
        keep, send = placed(scalars, pieces, columns)
        probe_grad, keep, send = lax.optimization_barrier((probe_grad, keep, send))
        previous = current
        probe_grad = sum_tiles(probe_grad)
        object_grad = keep + swap_modes(send)
        new_probe = ahead[-1] - probe_step * probe_grad
        if iteration < ITERS - 1:
            object_grad = object_grad + jnp.where(paired, swap_neighbours(object_grad), 0.0)
            parts = [
                object_grad[tile * 2 * size : (tile + 1) * 2 * size] for tile in range(columns)
            ]
            from_low, from_high = from_cols((parts[0], parts[-1]), swap_cols)
            parts[0] = parts[0] + from_low
            parts[-1] = parts[-1] + from_high
            current = [
                x - rate * g for x, rate, g in zip(ahead, rates, parts, strict=False)
            ] + [new_probe]
        else:
            object_grad = object_grad.reshape(columns, 2, size, size)
            given = jnp.where(lower, object_grad[:, :, half:], object_grad[:, :, :half])
            owned = jnp.where(lower, object_grad[:, :, :half], object_grad[:, :, half:])
            owned = owned + jnp.where(paired, swap_neighbours(given), 0.0)
            edges = (owned[0, :, :, :half], owned[-1, :, :, half:])
            from_low, from_high = from_cols(edges, swap_cols)
            owned = jnp.concatenate(
                [owned[0, :, :, half:] + from_low]
                + [owned[tile] for tile in range(1, columns - 1)]
                + [owned[-1, :, :, :half] + from_high],
                axis=2,
            )
            held = jnp.concatenate([x.reshape(2, size, size) for x in ahead[:-1]], axis=2)
            held = jnp.where(lower, held[:, :half], held[:, half:])
            strip = held[:, :, half : half + tile_cols] - object_rate * owned

    other = swap_modes(strip)
    whole = jnp.concatenate(
        [jnp.where(lower, other, strip), jnp.where(lower, strip, other)], axis=1
    )
    return (whole, new_probe.reshape(1, 2, size, size))


def solution(mesh):
    in_specs = (
        P(None, ("parts", "row"), "col"),
        P("mode", None, "parts", None),
        P("row", "col", "parts", None),
        P(("parts", "row"), "col"),
        P("row", "col", "parts", None, None),
    )
    out_specs = (P(None, ("parts", "row"), "col"), P("mode", None, "parts", None))
    return jax.shard_map(
        on_device, mesh=mesh, in_specs=in_specs, out_specs=out_specs, check_vma=False
    )
```

```python
import jax
import jax.numpy as jnp
import ml_dtypes
import numpy as np
from jax import lax
from jax.experimental import pallas as pl
from jax.experimental.pallas import tpu as pltpu
from jax.sharding import PartitionSpec as P

ITERS = 2


momentum = 0.5
object_rate = 0.1
probe_rate = 0.25

VMEM_LIMIT = 16 * 1024 * 1024


def transform_tables(size):
    half = size // 2
    point, freq = np.arange(half)[:, None], np.arange(half)[None, :]
    right, left, right_back, left_back = [], [], [], []
    for odd in range(2):
        angle = (point * (2 * freq + odd) % size) * (2.0 * np.pi / size)
        cosine, sine = np.cos(angle) / np.sqrt(size), np.sin(angle) / np.sqrt(size)
        table = np.block([[cosine, -sine], [sine, cosine]]).astype(np.float32)
        high = table.astype(ml_dtypes.bfloat16)
        low = (table - high.astype(np.float32)).astype(ml_dtypes.bfloat16)
        right.append(np.concatenate([high, low], axis=1))
        left.append(np.concatenate([high.T, low.T], axis=0))
        right_back.append(np.concatenate([high.T, low.T], axis=1))
        left_back.append(np.concatenate([high, low], axis=0))
    return [np.stack(t) for t in (right, left, left_back, right_back)]


def split(values):
    high = values.astype(jnp.bfloat16)
    return high, (values - high.astype(jnp.float32)).astype(jnp.bfloat16)


def matmul(left, right):
    return jnp.dot(left, right, preferred_element_type=jnp.float32)


def from_right(values, table):
    size = values.shape[1]
    both = matmul(
        jnp.concatenate(split(values), axis=1), jnp.concatenate([table, table], axis=0)
    )
    return both[:, :size] + both[:, size:]


def from_left(table, values):
    size = values.shape[0]
    both = matmul(
        jnp.concatenate([table, table], axis=1), jnp.concatenate(split(values), axis=0)
    )
    return both[:size] + both[size:]


def meld(first, second):
    half = first.shape[1] // 2
    low = lax.broadcasted_iota(jnp.int32, first.shape, 1) < half
    turned = pltpu.roll(jnp.where(low, second, first), half, 1)
    return jnp.where(low, first, turned), jnp.where(low, turned, second)


def stack_rows(*blocks):
    return jnp.concatenate(blocks, axis=0)


def stack_lanes(*blocks):
    return jnp.concatenate(blocks, axis=1)


def prepare_kernel(place, positions, counts, measured, order, root, windows, planes):
    slots, _, size, _ = measured.shape
    half = size // 2
    me = place[0]
    for index in range(slots):
        slot = 2 * index + me
        col = positions[1, slot] - place[3]
        windows[4 * index] = positions[0, slot] - place[2]
        windows[4 * index + 1] = col // size
        windows[4 * index + 2] = col % size
        windows[4 * index + 3] = (slot < counts[0, 0]).astype(jnp.int32)
    windows[4 * slots] = me
    windows[4 * slots + 1] = place[1]
    values = jnp.sqrt(measured[...].reshape(slots * size, size))
    high = values.astype(jnp.bfloat16)
    middle, low = split(values - high.astype(jnp.float32))
    planes[...] = matmul(high, order[...]) + (
        matmul(middle, order[...]) + matmul(low, order[...])
    )
    for index in range(slots):
        for odd in range(2):
            root[index, odd * half : (odd + 1) * half, :] = planes[
                pl.ds(index * size + odd, half, stride=2), :
            ]


def window_of(windows, index):
    return windows[4 * index], windows[4 * index + 1], windows[4 * index + 2]


def region(tile, half, size):
    return pl.ds(pl.multiple_of(tile * 2 * size + half * size, size), size)


def rows_of(row, tile, size):
    return pl.ds(tile * 2 * size + row, size)


def wave_kernel(windows, *refs, columns, group):
    mine, theirs = refs[: columns + 1], refs[columns + 1 : 2 * columns + 2]
    root, right, left, left_back, right_back = refs[2 * columns + 2 :][:5]
    keep, send, pieces, state, modes, grad = refs[2 * columns + 7 :]
    slots, size, _ = root.shape
    half = size // 2
    me, half_mine = windows[4 * slots], windows[4 * slots + 1]
    lane = lax.broadcasted_iota(jnp.int32, (size, size), 1)

    for blocks, side, mode in ((mine, half_mine, me), (theirs, 1 - half_mine, 1 - me)):
        for part in range(2):
            rows = slice(part * size, (part + 1) * size)
            for tile in range(columns):
                state[part, region(tile, side, size), :] = blocks[tile][rows, :]
        modes[mode] = blocks[-1][...]
    grad[...] = jnp.zeros_like(grad)

    def plane(mode, part):
        return modes[mode, part * size : (part + 1) * size, :]

    def one_group(first):
        patches, reals, imags = [], [], []
        for index in range(group):
            row, tile, shift = window_of(windows, first + index)
            patch = []
            for part in range(2):
                near = state[part, rows_of(row, tile, size), :]
                far = state[part, rows_of(row, tile + 1, size), :]
                patch.append(
                    pltpu.roll(jnp.where(lane >= shift, near, far), (size - shift) % size, 1)
                )
            patches.append(patch)
            for mode in range(2):
                real, imag = plane(mode, 0), plane(mode, 1)
                reals.append(real * patch[0] - imag * patch[1])
                imags.append(real * patch[1] + imag * patch[0])
        first_half, second_half = meld(stack_rows(*reals), stack_rows(*imags))
        real, imag = meld(
            from_right(first_half + second_half, right[0]),
            from_right(first_half - second_half, right[1]),
        )
        reals, imags = [], []
        for index in range(group):
            start = 2 * index * size
            both = [
                stack_lanes(x[start : start + size], x[start + size : start + 2 * size])
                for x in (real, imag)
            ]
            waves_back = []
            for odd in range(2):
                merged = [x[:half] - x[half:] if odd else x[:half] + x[half:] for x in both]
                far_field = from_left(left[odd], stack_rows(*merged))
                power = far_field * far_field
                power = power[:half] + power[half:]
                power = power[:, :size] + power[:, size:]
                live = windows[4 * (first + index) + 3].astype(jnp.float32)
                roots = root[first + index, odd * half : (odd + 1) * half, :]
                weight = (1.0 - roots * lax.rsqrt(power + 1.0)) * live
                weight = stack_lanes(weight, weight)
                waves_back.append(
                    from_left(left_back[odd], stack_rows(weight, weight) * far_field)
                )
            even, odd = waves_back
            sums, differences = even + odd, even - odd
            for mode in range(2):
                lanes = slice(mode * size, (mode + 1) * size)
                reals.append(stack_rows(sums[:half, lanes], differences[:half, lanes]))
                imags.append(stack_rows(sums[half:, lanes], differences[half:, lanes]))
        even, odd = meld(stack_rows(*reals), stack_rows(*imags))
        even, odd = from_right(even, right_back[0]), from_right(odd, right_back[1])
        real, imag = meld(even + odd, even - odd)
        for index in range(group):
            total = [0.0, 0.0]
            for mode in range(2):
                start = (2 * index + mode) * size
                chi_real, chi_imag = real[start : start + size], imag[start : start + size]
                probe_real, probe_imag = plane(mode, 0), plane(mode, 1)
                total[0] = total[0] + (probe_real * chi_real + probe_imag * chi_imag)
                total[1] = total[1] + (probe_real * chi_imag - probe_imag * chi_real)
                patch_real, patch_imag = patches[index]
                grad[mode, :size, :] += patch_real * chi_real + patch_imag * chi_imag
                grad[mode, size:, :] += patch_real * chi_imag - patch_imag * chi_real
            for part in range(2):
                pieces[first + index, part] = total[part]

    @pl.loop(0, slots // group)
    def _(step):
        one_group(step * group)

    keep[...] = grad[me]
    send[...] = grad[1 - me]


def place_kernel(windows, pieces, keep, send, grad, *, columns, owned_only):
    slots, _, size, _ = pieces.shape
    half_mine = windows[4 * slots + 1]
    lane = lax.broadcasted_iota(jnp.int32, (size, size), 1)
    grad[...] = jnp.zeros_like(grad)
    for index in range(slots):
        row, tile, shift = window_of(windows, index)
        inside = lane >= shift
        for part in range(2):
            turned = pltpu.roll(pieces[index, part], shift, 1)
            grad[part, rows_of(row, tile, size), :] += jnp.where(inside, turned, 0.0)
            grad[part, rows_of(row, tile + 1, size), :] += jnp.where(inside, 0.0, turned)
    cuts = 2 if owned_only else 1
    height = size // cuts
    for target, side in ((keep, half_mine), (send, 1 - half_mine)):
        for cut in range(cuts):
            for tile in range(columns):
                for part in range(2):
                    start = ((cut * columns + tile) * 2 + part) * height
                    skip = (side if cut == 0 else 1 - side) * height if owned_only else 0
                    first = tile * 2 * size + side * size + skip
                    rows = pl.ds(pl.multiple_of(first, height), height)
                    target[start : start + height, :] = grad[part, rows, :]


def whole_block(shape):
    return pl.BlockSpec(shape, lambda i, *_: (0,) * len(shape))


def prepared(place, positions, counts, measured):
    size = measured.shape[-1]
    slots = measured.shape[0] // 2
    order = np.zeros((size, size), ml_dtypes.bfloat16)
    order[np.concatenate([np.arange(0, size, 2), np.arange(1, size, 2)]), np.arange(size)] = 1
    return pl.pallas_call(
        prepare_kernel,
        out_shape=[
            jax.ShapeDtypeStruct((slots, size, size), jnp.float32),
            jax.ShapeDtypeStruct((4 * slots + 2,), jnp.int32),
        ],
        grid_spec=pltpu.PrefetchScalarGridSpec(
            num_scalar_prefetch=3,
            grid=(1,),
            in_specs=[
                pl.BlockSpec((slots, 1, size, size), lambda i, s, *_: (0, s[0], 0, 0)),
                whole_block((size, size)),
            ],
            out_specs=[
                whole_block((slots, size, size)),
                pl.BlockSpec(memory_space=pltpu.SMEM),
            ],
            scratch_shapes=[pltpu.VMEM((slots * size, size), jnp.float32)],
        ),
        compiler_params=pltpu.CompilerParams(vmem_limit_bytes=VMEM_LIMIT),
        cost_estimate=pl.CostEstimate(
            flops=6 * slots * size**3, bytes_accessed=8 * slots * size**2, transcendentals=0
        ),
        name="prepared",
    )(
        place,
        positions,
        counts,
        measured.reshape(slots, 2, size, size),
        jnp.asarray(order),
    )


def waves(windows, mine, theirs, root):
    slots, size, _ = root.shape
    columns = len(mine) - 1
    group = 4 if slots % 4 == 0 else 1
    pair = (2 * size, size)
    pieces = (slots, 2, size, size)
    tables = [jnp.asarray(t) for t in transform_tables(size)]

    def body(*refs):
        wave_kernel(*refs, columns=columns, group=group)

    return pl.pallas_call(
        body,
        out_shape=[jax.ShapeDtypeStruct(s, jnp.float32) for s in (pair, pair, pieces)],
        grid_spec=pltpu.PrefetchScalarGridSpec(
            num_scalar_prefetch=1,
            grid=(1,),
            in_specs=[whole_block(pair)] * (2 * columns + 2)
            + [whole_block(root.shape)]
            + [whole_block(t.shape) for t in tables],
            out_specs=[whole_block(s) for s in (pair, pair, pieces)],
            scratch_shapes=[
                pltpu.VMEM((2, columns * 2 * size, size), jnp.float32),
                pltpu.VMEM((2,) + pair, jnp.float32),
                pltpu.VMEM((2,) + pair, jnp.float32),
            ],
        ),
        compiler_params=pltpu.CompilerParams(vmem_limit_bytes=VMEM_LIMIT),
        name="waves",
    )(windows, *mine, *theirs, root, *tables)


def placed(windows, pieces, columns, owned_only):
    size = pieces.shape[-1]
    shape = (columns * 2 * size, size)

    def body(*refs):
        place_kernel(*refs, columns=columns, owned_only=owned_only)

    return pl.pallas_call(
        body,
        out_shape=[jax.ShapeDtypeStruct(shape, jnp.float32)] * 2,
        grid_spec=pltpu.PrefetchScalarGridSpec(
            num_scalar_prefetch=1,
            grid=(1,),
            in_specs=[whole_block(pieces.shape)],
            out_specs=[whole_block(shape)] * 2,
            scratch_shapes=[pltpu.VMEM((2,) + shape, jnp.float32)],
        ),
        compiler_params=pltpu.CompilerParams(vmem_limit_bytes=VMEM_LIMIT),
        name="placed",
    )(windows, pieces)


def swap_modes(block):
    return lax.ppermute(block, "mode", [(0, 1), (1, 0)])


def paired_with(index, parity, count):
    other = index + 1 if index % 2 == parity else index - 1
    return other if 0 <= other < count else None


def swap_neighbours(block, col_parity=None):
    rows, cols = lax.axis_size("row"), lax.axis_size("col")
    route = []
    for row in range(rows):
        for col in range(cols):
            for mode in range(2):
                to_row = paired_with(row, mode, rows)
                to_col = col if col_parity is None else paired_with(col, col_parity, cols)
                if to_col is None:
                    to_row, to_col = row, col
                elif to_row is None:
                    to_row = row
                    to_col = col ^ 1 if cols % 2 == 0 and col_parity is None else to_col
                route.append(
                    ((row * cols + col) * 2 + mode, (to_row * cols + to_col) * 2 + mode)
                )
    return lax.ppermute(block, ("row", "col", "mode"), route)


def from_cols(blocks, send):
    count = lax.axis_size("col")
    col = lax.axis_index("col")
    to_low, to_high = blocks
    from_low = from_high = jnp.zeros_like(to_low)
    for parity in range(min(2, count - 1)):
        is_low = col % 2 == parity
        got = send(jnp.where(is_low, to_high, to_low), parity)
        from_high = jnp.where(is_low & (col < count - 1), got, from_high)
        from_low = jnp.where(jnp.logical_not(is_low) & (col > 0), got, from_low)
    return from_low, from_high


def swap_cols(block, parity):
    count = lax.axis_size("col")
    others = [paired_with(i, parity, count) for i in range(count)]
    return lax.ppermute(block, "col", [(i, i if o is None else o) for i, o in enumerate(others)])


def sum_tiles(block):
    rows, cols = lax.axis_size("row"), lax.axis_size("col")
    along_cols = [(0, 1 << k) for k in range((cols - 1).bit_length())]
    along_rows = [(1 << k, 0) for k in range((rows - 1).bit_length())]
    if len(along_rows) > 1:
        turned = [(3, 0)] + along_cols + along_rows[:1] + along_rows[2:]
    else:
        turned = along_rows + along_cols
    for steps in zip(along_cols + along_rows, turned, strict=True):
        route = []
        for row in range(rows):
            for col in range(cols):
                for mode in range(2):
                    to_row, to_col = row ^ steps[mode][0], col ^ steps[mode][1]
                    route.append(
                        ((row * cols + col) * 2 + mode, (to_row * cols + to_col) * 2 + mode)
                    )
        block = block + lax.ppermute(block, ("row", "col", "mode"), route)
    return block


def on_device(obj, probe, positions, counts, measured):
    size = probe.shape[-1]
    half = size // 2
    tile_rows, tile_cols = obj.shape[1:]
    columns = tile_cols // size + 1
    slot_count = positions.shape[2]
    rows_count, cols_count = lax.axis_size("row"), lax.axis_size("col")
    me = lax.axis_index("mode")
    row = lax.axis_index("row")
    col = lax.axis_index("col")
    lower = row % 2 == me
    paired = jnp.where(lower, row < rows_count - 1, row > 0)
    half_mine = lower.astype(jnp.int32)
    place = jnp.stack(
        [me, half_mine, row * tile_rows - half, col * tile_cols - half]
    ).astype(jnp.int32)
    root, windows = prepared(place, positions[0, 0].T, counts, measured[0, 0])
    probe_step = probe_rate / (slot_count * rows_count * cols_count)

    strip = jnp.where(lower, obj[:, half:], obj[:, :half])
    edges = (strip[:, :, :half], strip[:, :, tile_cols - half :])
    beside = swap_neighbours(strip)
    strip_low, strip_high = from_cols(edges, swap_cols)
    corner_low, corner_high = from_cols(edges, swap_neighbours)
    beside, root, windows = lax.optimization_barrier((beside, root, windows))
    strip = jnp.concatenate([strip_low, strip, strip_high], axis=2)
    beside = jnp.concatenate([corner_low, beside, corner_high], axis=2)
    beside = jnp.where(paired, beside, 0.0)
    wide = jnp.concatenate(
        [jnp.where(lower, strip, beside), jnp.where(lower, beside, strip)], axis=1
    )
    start = [
        wide[:, :, tile * size : (tile + 1) * size].reshape(2 * size, size)
        for tile in range(columns)
    ] + [probe[0].reshape(2 * size, size)]

    ext_rows = jnp.arange(size, dtype=jnp.int32)[:, None] + half_mine * size - half
    ext_rows = jnp.concatenate([ext_rows, ext_rows]) + row * tile_rows
    rows_inside = (ext_rows >= 0) & (ext_rows < tile_rows * rows_count)
    rates = []
    for tile in range(columns):
        ext_cols = jnp.arange(size, dtype=jnp.int32)[None, :] + tile * size - half + col * tile_cols
        inside = rows_inside & (ext_cols >= 0) & (ext_cols < tile_cols * cols_count)
        rates.append(jnp.where(inside, jnp.float32(object_rate), 0.0))

    previous, current = start, start
    ahead, others = start, [swap_modes(x) for x in start]
    for iteration in range(ITERS):
        keep, send, pieces = waves(windows, ahead, others, root)
        probe_grad = keep + swap_modes(send)
        keep, send = placed(windows, pieces, columns, iteration == ITERS - 1)
        probe_grad, keep, send = lax.optimization_barrier((probe_grad, keep, send))
        previous = current
        probe_grad = sum_tiles(probe_grad)
        object_grad = keep + swap_modes(send)
        if iteration < ITERS - 1:
            object_grad = object_grad + jnp.where(paired, swap_neighbours(object_grad), 0.0)
            parts = [
                object_grad[tile * 2 * size : (tile + 1) * 2 * size] for tile in range(columns)
            ]
            from_low, from_high = from_cols((parts[0], parts[-1]), swap_cols)
            parts[0] = parts[0] + from_low
            parts[-1] = parts[-1] + from_high
            current = [x - rate * g for x, rate, g in zip(ahead, rates, parts, strict=False)]
            tiles = [x + momentum * (x - y) for x, y in zip(current, previous, strict=False)]
            others = [swap_modes(x) for x in tiles]
            new_probe = ahead[-1] - probe_step * probe_grad
            current = current + [new_probe]
            ahead = tiles + [new_probe + momentum * (new_probe - previous[-1])]
            others = others + [swap_modes(ahead[-1])]
        else:
            object_grad = object_grad.reshape(2, columns, 2, half, size)
            given, owned = object_grad[0], object_grad[1]
            owned = owned + jnp.where(paired, swap_neighbours(given), 0.0)
            edges = (owned[0, :, :, :half], owned[-1, :, :, half:])
            from_low, from_high = from_cols(edges, swap_cols)
            owned = jnp.concatenate(
                [owned[0, :, :, half:] + from_low]
                + [owned[tile] for tile in range(1, columns - 1)]
                + [owned[-1, :, :, :half] + from_high],
                axis=2,
            )
            held = jnp.concatenate([x.reshape(2, size, size) for x in ahead[:-1]], axis=2)
            held = jnp.where(lower, held[:, :half], held[:, half:])
            strip = held[:, :, half : half + tile_cols] - object_rate * owned

    other = swap_modes(strip)
    whole = jnp.concatenate(
        [jnp.where(lower, other, strip), jnp.where(lower, strip, other)], axis=1
    )
    new_probe = ahead[-1] - probe_step * probe_grad
    return (whole, new_probe.reshape(1, 2, size, size))


def solution(mesh):
    in_specs = (
        P(None, ("parts", "row"), "col"),
        P("mode", None, "parts", None),
        P("row", "col", "parts", None),
        P(("parts", "row"), "col"),
        P("row", "col", "parts", None, None),
    )
    out_specs = (P(None, ("parts", "row"), "col"), P("mode", None, "parts", None))
    return jax.shard_map(
        on_device, mesh=mesh, in_specs=in_specs, out_specs=out_specs, check_vma=False
    )
```

```python
import math

import jax
import jax.numpy as jnp
import ml_dtypes
import numpy as np
from jax import lax
from jax.experimental import pallas as pl
from jax.experimental.pallas import tpu as pltpu
from jax.sharding import PartitionSpec as P

ITERS = 2


momentum = 0.5
object_rate = 0.1
probe_rate = 0.25

VMEM_LIMIT = 16 * 1024 * 1024


def transform_tables(size):
    half = size // 2
    point, freq = np.arange(half)[:, None], np.arange(half)[None, :]
    right, left, right_back, left_back = [], [], [], []
    for odd in range(2):
        angle = (point * (2 * freq + odd) % size) * (2.0 * np.pi / size)
        cosine, sine = np.cos(angle) / np.sqrt(size), np.sin(angle) / np.sqrt(size)
        table = np.block([[cosine, -sine], [sine, cosine]]).astype(np.float32)
        high = table.astype(ml_dtypes.bfloat16)
        low = (table - high.astype(np.float32)).astype(ml_dtypes.bfloat16)
        right.append(np.concatenate([high, low], axis=1))
        left.append(np.concatenate([high.T, low.T], axis=0))
        right_back.append(np.concatenate([high.T, low.T], axis=1))
        left_back.append(np.concatenate([high, low], axis=0))
    return [np.stack(t) for t in (right, left, left_back, right_back)]


def split(values):
    high = values.astype(jnp.bfloat16)
    return high, (values - high.astype(jnp.float32)).astype(jnp.bfloat16)


def matmul(left, right):
    return jnp.dot(left, right, preferred_element_type=jnp.float32)


def from_right(values, table):
    size = values.shape[1]
    both = matmul(
        jnp.concatenate(split(values), axis=1), jnp.concatenate([table, table], axis=0)
    )
    return both[:, :size] + both[:, size:]


def from_left(table, values):
    size = values.shape[0]
    both = matmul(
        jnp.concatenate([table, table], axis=1), jnp.concatenate(split(values), axis=0)
    )
    return both[:size] + both[size:]


def meld(first, second):
    half = first.shape[1] // 2
    low = lax.broadcasted_iota(jnp.int32, first.shape, 1) < half
    turned = pltpu.roll(jnp.where(low, second, first), half, 1)
    return jnp.where(low, first, turned), jnp.where(low, turned, second)


def stack_rows(*blocks):
    return jnp.concatenate(blocks, axis=0)


def stack_lanes(*blocks):
    return jnp.concatenate(blocks, axis=1)


def prepare_kernel(place, positions, counts, measured, order, root, windows, planes):
    slots, _, size, _ = measured.shape
    half = size // 2
    me = place[0]
    for index in range(slots):
        slot = 2 * index + me
        col = positions[1, slot] - place[3]
        windows[4 * index] = positions[0, slot] - place[2]
        windows[4 * index + 1] = col // size
        windows[4 * index + 2] = col % size
        windows[4 * index + 3] = (slot < counts[0, 0]).astype(jnp.int32)
    windows[4 * slots] = me
    windows[4 * slots + 1] = place[1]
    values = jnp.sqrt(measured[...].reshape(slots * size, size))
    high = values.astype(jnp.bfloat16)
    middle, low = split(values - high.astype(jnp.float32))
    planes[...] = matmul(high, order[...]) + (
        matmul(middle, order[...]) + matmul(low, order[...])
    )
    for index in range(slots):
        for odd in range(2):
            root[index, odd * half : (odd + 1) * half, :] = planes[
                pl.ds(index * size + odd, half, stride=2), :
            ]


def window_of(windows, index):
    return windows[4 * index], windows[4 * index + 1], windows[4 * index + 2]


def region(tile, half, size):
    return pl.ds(pl.multiple_of(tile * 2 * size + half * size, size), size)


def rows_of(row, tile, size):
    return pl.ds(tile * 2 * size + row, size)


def wave_kernel(windows, *refs, columns, group):
    mine, theirs = refs[:2], refs[2:4]
    root, right, left, left_back, right_back = refs[4:9]
    keep, send, pieces, state, modes, grad = refs[9:]
    slots, size, _ = root.shape
    half = size // 2
    me, half_mine = windows[4 * slots], windows[4 * slots + 1]
    lane = lax.broadcasted_iota(jnp.int32, (size, size), 1)

    for blocks, side, mode in ((mine, half_mine, me), (theirs, 1 - half_mine, 1 - me)):
        for part in range(2):
            for tile in range(columns):
                start = (2 * tile + part) * size
                state[part, region(tile, side, size), :] = blocks[0][start : start + size, :]
        modes[mode] = blocks[1][...]
    grad[...] = jnp.zeros_like(grad)

    def plane(mode, part):
        return modes[mode, part * size : (part + 1) * size, :]

    def one_group(first):
        patches, reals, imags = [], [], []
        for index in range(group):
            row, tile, shift = window_of(windows, first + index)
            patch = []
            for part in range(2):
                near = state[part, rows_of(row, tile, size), :]
                far = state[part, rows_of(row, tile + 1, size), :]
                patch.append(
                    pltpu.roll(jnp.where(lane >= shift, near, far), (size - shift) % size, 1)
                )
            patches.append(patch)
            for mode in range(2):
                real, imag = plane(mode, 0), plane(mode, 1)
                reals.append(real * patch[0] - imag * patch[1])
                imags.append(real * patch[1] + imag * patch[0])
        first_half, second_half = meld(stack_rows(*reals), stack_rows(*imags))
        real, imag = meld(
            from_right(first_half + second_half, right[0]),
            from_right(first_half - second_half, right[1]),
        )
        reals, imags = [], []
        for index in range(group):
            start = 2 * index * size
            both = [
                stack_lanes(x[start : start + size], x[start + size : start + 2 * size])
                for x in (real, imag)
            ]
            waves_back = []
            for odd in range(2):
                merged = [x[:half] - x[half:] if odd else x[:half] + x[half:] for x in both]
                far_field = from_left(left[odd], stack_rows(*merged))
                power = far_field * far_field
                power = power[:half] + power[half:]
                power = power[:, :size] + power[:, size:]
                live = windows[4 * (first + index) + 3].astype(jnp.float32)
                roots = root[first + index, odd * half : (odd + 1) * half, :]
                weight = (1.0 - roots * lax.rsqrt(power + 1.0)) * live
                weight = stack_lanes(weight, weight)
                waves_back.append(
                    from_left(left_back[odd], stack_rows(weight, weight) * far_field)
                )
            even, odd = waves_back
            sums, differences = even + odd, even - odd
            for mode in range(2):
                lanes = slice(mode * size, (mode + 1) * size)
                reals.append(stack_rows(sums[:half, lanes], differences[:half, lanes]))
                imags.append(stack_rows(sums[half:, lanes], differences[half:, lanes]))
        even, odd = meld(stack_rows(*reals), stack_rows(*imags))
        even, odd = from_right(even, right_back[0]), from_right(odd, right_back[1])
        real, imag = meld(even + odd, even - odd)
        for index in range(group):
            total = [0.0, 0.0]
            for mode in range(2):
                start = (2 * index + mode) * size
                chi_real, chi_imag = real[start : start + size], imag[start : start + size]
                probe_real, probe_imag = plane(mode, 0), plane(mode, 1)
                total[0] = total[0] + (probe_real * chi_real + probe_imag * chi_imag)
                total[1] = total[1] + (probe_real * chi_imag - probe_imag * chi_real)
                patch_real, patch_imag = patches[index]
                grad[mode, :size, :] += patch_real * chi_real + patch_imag * chi_imag
                grad[mode, size:, :] += patch_real * chi_imag - patch_imag * chi_real
            for part in range(2):
                pieces[first + index, part] = total[part]

    @pl.loop(0, slots // group)
    def _(step):
        one_group(step * group)

    keep[...] = grad[me]
    send[...] = grad[1 - me]


def place_kernel(windows, pieces, keep, send, grad, *, columns, owned_only):
    slots, _, size, _ = pieces.shape
    half_mine = windows[4 * slots + 1]
    lane = lax.broadcasted_iota(jnp.int32, (size, size), 1)
    grad[...] = jnp.zeros_like(grad)
    for index in range(slots):
        row, tile, shift = window_of(windows, index)
        inside = lane >= shift
        for part in range(2):
            turned = pltpu.roll(pieces[index, part], shift, 1)
            grad[part, rows_of(row, tile, size), :] += jnp.where(inside, turned, 0.0)
            grad[part, rows_of(row, tile + 1, size), :] += jnp.where(inside, 0.0, turned)
    cuts = 2 if owned_only else 1
    height = size // cuts
    for target, side in ((keep, half_mine), (send, 1 - half_mine)):
        for cut in range(cuts):
            for tile in range(columns):
                for part in range(2):
                    start = ((cut * columns + tile) * 2 + part) * height
                    skip = (side if cut == 0 else 1 - side) * height if owned_only else 0
                    first = tile * 2 * size + side * size + skip
                    rows = pl.ds(pl.multiple_of(first, height), height)
                    target[start : start + height, :] = grad[part, rows, :]


def whole_block(shape):
    return pl.BlockSpec(shape, lambda i, *_: (0,) * len(shape))


def prepared(place, positions, counts, measured):
    size = measured.shape[-1]
    slots = measured.shape[0] // 2
    order = np.zeros((size, size), ml_dtypes.bfloat16)
    order[np.concatenate([np.arange(0, size, 2), np.arange(1, size, 2)]), np.arange(size)] = 1
    return pl.pallas_call(
        prepare_kernel,
        out_shape=[
            jax.ShapeDtypeStruct((slots, size, size), jnp.float32),
            jax.ShapeDtypeStruct((4 * slots + 2,), jnp.int32),
        ],
        grid_spec=pltpu.PrefetchScalarGridSpec(
            num_scalar_prefetch=3,
            grid=(1,),
            in_specs=[
                pl.BlockSpec((slots, 1, size, size), lambda i, s, *_: (0, s[0], 0, 0)),
                whole_block((size, size)),
            ],
            out_specs=[
                whole_block((slots, size, size)),
                pl.BlockSpec(memory_space=pltpu.SMEM),
            ],
            scratch_shapes=[pltpu.VMEM((slots * size, size), jnp.float32)],
        ),
        compiler_params=pltpu.CompilerParams(vmem_limit_bytes=VMEM_LIMIT),
        cost_estimate=pl.CostEstimate(
            flops=6 * slots * size**3, bytes_accessed=8 * slots * size**2, transcendentals=0
        ),
        name="prepared",
    )(
        place,
        positions,
        counts,
        measured.reshape(slots, 2, size, size),
        jnp.asarray(order),
    )


def waves(windows, mine, theirs, root):
    slots, size, _ = root.shape
    columns = mine[0].shape[0] // (2 * size)
    group = slots if slots <= 8 else math.gcd(slots, 4)
    pair = (2 * size, size)
    pieces = (slots, 2, size, size)
    tables = [jnp.asarray(t) for t in transform_tables(size)]

    def body(*refs):
        wave_kernel(*refs, columns=columns, group=group)

    return pl.pallas_call(
        body,
        out_shape=[jax.ShapeDtypeStruct(s, jnp.float32) for s in (pair, pair, pieces)],
        grid_spec=pltpu.PrefetchScalarGridSpec(
            num_scalar_prefetch=1,
            grid=(1,),
            in_specs=[whole_block(mine[0].shape), whole_block(pair)] * 2
            + [whole_block(root.shape)]
            + [whole_block(t.shape) for t in tables],
            out_specs=[whole_block(s) for s in (pair, pair, pieces)],
            scratch_shapes=[
                pltpu.VMEM((2, columns * 2 * size, size), jnp.float32),
                pltpu.VMEM((2,) + pair, jnp.float32),
                pltpu.VMEM((2,) + pair, jnp.float32),
            ],
        ),
        compiler_params=pltpu.CompilerParams(vmem_limit_bytes=VMEM_LIMIT),
        name="waves",
    )(windows, *mine, *theirs, root, *tables)


def placed(windows, pieces, columns, owned_only):
    size = pieces.shape[-1]
    shape = (columns * 2 * size, size)

    def body(*refs):
        place_kernel(*refs, columns=columns, owned_only=owned_only)

    return pl.pallas_call(
        body,
        out_shape=[jax.ShapeDtypeStruct(shape, jnp.float32)] * 2,
        grid_spec=pltpu.PrefetchScalarGridSpec(
            num_scalar_prefetch=1,
            grid=(1,),
            in_specs=[whole_block(pieces.shape)],
            out_specs=[whole_block(shape)] * 2,
            scratch_shapes=[pltpu.VMEM((2,) + shape, jnp.float32)],
        ),
        compiler_params=pltpu.CompilerParams(vmem_limit_bytes=VMEM_LIMIT),
        name="placed",
    )(windows, pieces)


def swap_modes(block):
    return lax.ppermute(block, "mode", [(0, 1), (1, 0)])


def paired_with(index, parity, count):
    other = index + 1 if index % 2 == parity else index - 1
    return other if 0 <= other < count else None


def swap_neighbours(block, col_parity=None):
    rows, cols = lax.axis_size("row"), lax.axis_size("col")
    route = []
    for row in range(rows):
        for col in range(cols):
            for mode in range(2):
                to_row = paired_with(row, mode, rows)
                to_col = col if col_parity is None else paired_with(col, col_parity, cols)
                if to_col is None:
                    to_row, to_col = row, col
                elif to_row is None:
                    to_row = row
                    to_col = col ^ 1 if cols % 2 == 0 and col_parity is None else to_col
                route.append(
                    ((row * cols + col) * 2 + mode, (to_row * cols + to_col) * 2 + mode)
                )
    return lax.ppermute(block, ("row", "col", "mode"), route)


def from_cols(blocks, send):
    count = lax.axis_size("col")
    col = lax.axis_index("col")
    to_low, to_high = blocks
    from_low = from_high = jnp.zeros_like(to_low)
    for parity in range(min(2, count - 1)):
        is_low = col % 2 == parity
        got = send(jnp.where(is_low, to_high, to_low), parity)
        from_high = jnp.where(is_low & (col < count - 1), got, from_high)
        from_low = jnp.where(jnp.logical_not(is_low) & (col > 0), got, from_low)
    return from_low, from_high


def swap_cols(block, parity):
    count = lax.axis_size("col")
    others = [paired_with(i, parity, count) for i in range(count)]
    return lax.ppermute(block, "col", [(i, i if o is None else o) for i, o in enumerate(others)])


def tile_sum_stages(beside_little):
    rows, cols = lax.axis_size("row"), lax.axis_size("col")
    if beside_little and (rows, cols) == (4, 2):
        first = [[(0, 1)], [(2, 0), (1, 0), (3, 0)]]
        second = [[(3, 0)], [(0, 1), (1, 0), (1, 1)]]
    else:
        along_cols = [[(0, 1 << k)] for k in range((cols - 1).bit_length())]
        along_rows = [[(1 << k, 0)] for k in range((rows - 1).bit_length())]
        first = along_cols + along_rows
        second = along_rows + along_cols
        if len(along_rows) > 1:
            second = [[(3, 0)]] + along_cols + along_rows[:1] + along_rows[2:]
    return [list(zip(*stage, strict=True)) for stage in zip(first, second, strict=True)]


def sum_tiles(block, stages):
    sums = []
    rows, cols = lax.axis_size("row"), lax.axis_size("col")
    for stage in stages:
        arrived = []
        for flips in stage:
            route = []
            for row in range(rows):
                for col in range(cols):
                    for mode in range(2):
                        to_row, to_col = row ^ flips[mode][0], col ^ flips[mode][1]
                        route.append(
                            ((row * cols + col) * 2 + mode, (to_row * cols + to_col) * 2 + mode)
                        )
            arrived.append(lax.ppermute(block, ("row", "col", "mode"), route))
        block = sum(arrived, start=block)
        sums.append(block)
    return sums


def on_device(obj, probe, positions, counts, measured):
    size = probe.shape[-1]
    half = size // 2
    tile_rows, tile_cols = obj.shape[1:]
    columns = tile_cols // size + 1
    slot_count = positions.shape[2]
    rows_count, cols_count = lax.axis_size("row"), lax.axis_size("col")
    me = lax.axis_index("mode")
    row = lax.axis_index("row")
    col = lax.axis_index("col")
    lower = row % 2 == me
    paired = jnp.where(lower, row < rows_count - 1, row > 0)
    half_mine = lower.astype(jnp.int32)
    place = jnp.stack(
        [me, half_mine, row * tile_rows - half, col * tile_cols - half]
    ).astype(jnp.int32)
    root, windows = prepared(place, positions[0, 0].T, counts, measured[0, 0])
    probe_step = probe_rate / (slot_count * rows_count * cols_count)

    strip = jnp.where(lower, obj[:, half:], obj[:, :half])
    edges = (strip[:, :, :half], strip[:, :, tile_cols - half :])
    beside = swap_neighbours(strip)
    strip_low, strip_high = from_cols(edges, swap_cols)
    corner_low, corner_high = from_cols(edges, swap_neighbours)
    beside, root, windows = lax.optimization_barrier((beside, root, windows))
    strip = jnp.concatenate([strip_low, strip, strip_high], axis=2)
    beside = jnp.concatenate([corner_low, beside, corner_high], axis=2)
    beside = jnp.where(paired, beside, 0.0)
    wide = jnp.concatenate(
        [jnp.where(lower, strip, beside), jnp.where(lower, beside, strip)], axis=1
    )
    tiles = [wide[:, :, tile * size : (tile + 1) * size] for tile in range(columns)]
    start = [
        jnp.concatenate(tiles).reshape(columns * 2 * size, size),
        probe[0].reshape(2 * size, size),
    ]

    ext_rows = jnp.arange(size, dtype=jnp.int32)[:, None] + half_mine * size - half
    ext_rows = jnp.concatenate([ext_rows, ext_rows]) + row * tile_rows
    rows_inside = (ext_rows >= 0) & (ext_rows < tile_rows * rows_count)
    rates = []
    for tile in range(columns):
        ext_cols = jnp.arange(size, dtype=jnp.int32)[None, :] + tile * size - half + col * tile_cols
        inside = rows_inside & (ext_cols >= 0) & (ext_cols < tile_cols * cols_count)
        rates.append(jnp.where(inside, jnp.float32(object_rate), 0.0))

    rates = jnp.concatenate(rates)
    previous, current = start, start
    ahead, others = start, [swap_modes(x) for x in start]
    for iteration in range(ITERS):
        keep, send, pieces = waves(windows, ahead, others, root)
        probe_grad = keep + swap_modes(send)
        keep, send = placed(windows, pieces, columns, iteration == ITERS - 1)
        probe_grad, keep, send = lax.optimization_barrier((probe_grad, keep, send))
        previous = current
        sums = sum_tiles(probe_grad, tile_sum_stages(iteration == ITERS - 1))
        probe_grad = sums[-1]
        object_grad = keep + swap_modes(send)
        if iteration < ITERS - 1:
            object_grad = object_grad + jnp.where(paired, swap_neighbours(object_grad), 0.0)
            object_grad, _ = lax.optimization_barrier((object_grad, sums[1]))
            parts = [
                object_grad[tile * 2 * size : (tile + 1) * 2 * size] for tile in range(columns)
            ]
            from_low, from_high = from_cols((parts[0], parts[-1]), swap_cols)
            parts[0] = parts[0] + from_low
            parts[-1] = parts[-1] + from_high
            new_object = ahead[0] - rates * jnp.concatenate(parts)
            probe_grad, new_object = lax.optimization_barrier((probe_grad, new_object))
            new_probe = ahead[1] - probe_step * probe_grad
            current = [new_object, new_probe]
            ahead = [x + momentum * (x - y) for x, y in zip(current, previous, strict=True)]
            others = [swap_modes(x) for x in ahead]
        else:
            object_grad = object_grad.reshape(2, columns, 2, half, size)
            given, owned = object_grad[0], object_grad[1]
            owned = owned + jnp.where(paired, swap_neighbours(given), 0.0)
            edges = (owned[0, :, :, :half], owned[-1, :, :, half:])
            from_low, from_high = from_cols(edges, swap_cols)
            owned = jnp.concatenate(
                [owned[0, :, :, half:] + from_low]
                + [owned[tile] for tile in range(1, columns - 1)]
                + [owned[-1, :, :, :half] + from_high],
                axis=2,
            )
            held = ahead[0].reshape(columns, 2, size, size)
            held = jnp.concatenate([held[tile] for tile in range(columns)], axis=2)
            held = jnp.where(lower, held[:, :half], held[:, half:])
            strip = held[:, :, half : half + tile_cols] - object_rate * owned

    other = swap_modes(strip)
    whole = jnp.concatenate(
        [jnp.where(lower, other, strip), jnp.where(lower, strip, other)], axis=1
    )
    new_probe = ahead[-1] - probe_step * probe_grad
    return (whole, new_probe.reshape(1, 2, size, size))


def solution(mesh):
    in_specs = (
        P(None, ("parts", "row"), "col"),
        P("mode", None, "parts", None),
        P("row", "col", "parts", None),
        P(("parts", "row"), "col"),
        P("row", "col", "parts", None, None),
    )
    out_specs = (P(None, ("parts", "row"), "col"), P("mode", None, "parts", None))
    return jax.shard_map(
        on_device, mesh=mesh, in_specs=in_specs, out_specs=out_specs, check_vma=False
    )
```

```python
import math

import jax
import jax.numpy as jnp
import ml_dtypes
import numpy as np
from jax import lax
from jax.experimental import pallas as pl
from jax.experimental.pallas import tpu as pltpu
from jax.sharding import PartitionSpec as P

ITERS = 2


momentum = 0.5
object_rate = 0.1
probe_rate = 0.25

VMEM_LIMIT = 16 * 1024 * 1024


def transform_tables(size):
    half = size // 2
    point, freq = np.arange(half)[:, None], np.arange(half)[None, :]
    right, left, right_back, left_back = [], [], [], []
    for odd in range(2):
        angle = (point * (2 * freq + odd) % size) * (2.0 * np.pi / size)
        cosine, sine = np.cos(angle) / np.sqrt(size), np.sin(angle) / np.sqrt(size)
        table = np.block([[cosine, -sine], [sine, cosine]]).astype(np.float32)
        high = table.astype(ml_dtypes.bfloat16)
        low = (table - high.astype(np.float32)).astype(ml_dtypes.bfloat16)
        right.append(np.concatenate([high, low], axis=1))
        left.append(np.concatenate([high.T, low.T], axis=0))
        right_back.append(np.concatenate([high.T, low.T], axis=1))
        left_back.append(np.concatenate([high, low], axis=0))
    return [np.stack(t) for t in (right, left, left_back, right_back)]


def split(values):
    high = values.astype(jnp.bfloat16)
    return high, (values - high.astype(jnp.float32)).astype(jnp.bfloat16)


def matmul(left, right):
    return jnp.dot(left, right, preferred_element_type=jnp.float32)


def from_right(values, table):
    size = values.shape[1]
    both = matmul(
        jnp.concatenate(split(values), axis=1), jnp.concatenate([table, table], axis=0)
    )
    return both[:, :size] + both[:, size:]


def from_left(table, values):
    size = values.shape[0]
    both = matmul(
        jnp.concatenate([table, table], axis=1), jnp.concatenate(split(values), axis=0)
    )
    return both[:size] + both[size:]


def meld(first, second):
    half = first.shape[1] // 2
    low = lax.broadcasted_iota(jnp.int32, first.shape, 1) < half
    turned = pltpu.roll(jnp.where(low, second, first), half, 1)
    return jnp.where(low, first, turned), jnp.where(low, turned, second)


def stack_rows(*blocks):
    return jnp.concatenate(blocks, axis=0)


def stack_lanes(*blocks):
    return jnp.concatenate(blocks, axis=1)


def prepare_kernel(place, positions, counts, measured, order, root, windows, planes):
    slots, _, size, _ = measured.shape
    half = size // 2
    me = place[0]
    for index in range(slots):
        slot = 2 * index + me
        col = positions[1, slot] - place[3]
        windows[4 * index] = positions[0, slot] - place[2]
        windows[4 * index + 1] = col // size
        windows[4 * index + 2] = col % size
        windows[4 * index + 3] = (slot < counts[0, 0]).astype(jnp.int32)
    windows[4 * slots] = me
    windows[4 * slots + 1] = place[1]
    values = jnp.sqrt(measured[...].reshape(slots * size, size))
    high = values.astype(jnp.bfloat16)
    middle, low = split(values - high.astype(jnp.float32))
    planes[...] = matmul(high, order[...]) + (
        matmul(middle, order[...]) + matmul(low, order[...])
    )
    for index in range(slots):
        for odd in range(2):
            root[index, odd * half : (odd + 1) * half, :] = planes[
                pl.ds(index * size + odd, half, stride=2), :
            ]


def window_of(windows, index):
    return windows[4 * index], windows[4 * index + 1], windows[4 * index + 2]


def region(tile, half, size):
    return pl.ds(pl.multiple_of(tile * 2 * size + half * size, size), size)


def rows_of(row, tile, size):
    return pl.ds(tile * 2 * size + row, size)


def wave_kernel(windows, *refs, columns, group):
    mine, theirs = refs[:2], refs[2:4]
    root, right, left, left_back, right_back = refs[4:9]
    keep, send, pieces, state, modes, grad = refs[9:]
    slots, size, _ = root.shape
    half = size // 2
    me, half_mine = windows[4 * slots], windows[4 * slots + 1]
    lane = lax.broadcasted_iota(jnp.int32, (size, size), 1)

    for blocks, side, mode in ((mine, half_mine, me), (theirs, 1 - half_mine, 1 - me)):
        for part in range(2):
            for tile in range(columns):
                start = (2 * tile + part) * size
                state[part, region(tile, side, size), :] = blocks[0][start : start + size, :]
        modes[mode] = blocks[1][...]
    grad[...] = jnp.zeros_like(grad)

    def plane(mode, part):
        return modes[mode, part * size : (part + 1) * size, :]

    def one_group(first):
        patches, reals, imags = [], [], []
        for index in range(group):
            row, tile, shift = window_of(windows, first + index)
            patch = []
            for part in range(2):
                near = state[part, rows_of(row, tile, size), :]
                far = state[part, rows_of(row, tile + 1, size), :]
                patch.append(
                    pltpu.roll(jnp.where(lane >= shift, near, far), (size - shift) % size, 1)
                )
            patches.append(patch)
            for mode in range(2):
                real, imag = plane(mode, 0), plane(mode, 1)
                reals.append(real * patch[0] - imag * patch[1])
                imags.append(real * patch[1] + imag * patch[0])
        first_half, second_half = meld(stack_rows(*reals), stack_rows(*imags))
        real, imag = meld(
            from_right(first_half + second_half, right[0]),
            from_right(first_half - second_half, right[1]),
        )
        reals, imags = [], []
        for index in range(group):
            start = 2 * index * size
            both = [
                stack_lanes(x[start : start + size], x[start + size : start + 2 * size])
                for x in (real, imag)
            ]
            waves_back = []
            for odd in range(2):
                merged = [x[:half] - x[half:] if odd else x[:half] + x[half:] for x in both]
                far_field = from_left(left[odd], stack_rows(*merged))
                power = far_field * far_field
                power = power[:half] + power[half:]
                power = power[:, :size] + power[:, size:]
                live = windows[4 * (first + index) + 3].astype(jnp.float32)
                roots = root[first + index, odd * half : (odd + 1) * half, :]
                weight = (1.0 - roots * lax.rsqrt(power + 1.0)) * live
                weight = stack_lanes(weight, weight)
                waves_back.append(
                    from_left(left_back[odd], stack_rows(weight, weight) * far_field)
                )
            even, odd = waves_back
            sums, differences = even + odd, even - odd
            for mode in range(2):
                lanes = slice(mode * size, (mode + 1) * size)
                reals.append(stack_rows(sums[:half, lanes], differences[:half, lanes]))
                imags.append(stack_rows(sums[half:, lanes], differences[half:, lanes]))
        even, odd = meld(stack_rows(*reals), stack_rows(*imags))
        even, odd = from_right(even, right_back[0]), from_right(odd, right_back[1])
        real, imag = meld(even + odd, even - odd)
        for index in range(group):
            total = [0.0, 0.0]
            for mode in range(2):
                start = (2 * index + mode) * size
                chi_real, chi_imag = real[start : start + size], imag[start : start + size]
                probe_real, probe_imag = plane(mode, 0), plane(mode, 1)
                total[0] = total[0] + (probe_real * chi_real + probe_imag * chi_imag)
                total[1] = total[1] + (probe_real * chi_imag - probe_imag * chi_real)
                patch_real, patch_imag = patches[index]
                grad[mode, :size, :] += patch_real * chi_real + patch_imag * chi_imag
                grad[mode, size:, :] += patch_real * chi_imag - patch_imag * chi_real
            for part in range(2):
                pieces[first + index, part] = total[part]

    @pl.loop(0, slots // group)
    def _(step):
        one_group(step * group)

    keep[...] = grad[me]
    send[...] = grad[1 - me]


def place_kernel(windows, pieces, keep, send, grad, *, columns, owned_only):
    slots, _, size, _ = pieces.shape
    half_mine = windows[4 * slots + 1]
    lane = lax.broadcasted_iota(jnp.int32, (size, size), 1)
    grad[...] = jnp.zeros_like(grad)
    for index in range(slots):
        row, tile, shift = window_of(windows, index)
        inside = lane >= shift
        for part in range(2):
            turned = pltpu.roll(pieces[index, part], shift, 1)
            grad[part, rows_of(row, tile, size), :] += jnp.where(inside, turned, 0.0)
            grad[part, rows_of(row, tile + 1, size), :] += jnp.where(inside, 0.0, turned)
    cuts = 2 if owned_only else 1
    height = size // cuts
    for target, side in ((keep, half_mine), (send, 1 - half_mine)):
        for cut in range(cuts):
            for tile in range(columns):
                for part in range(2):
                    start = ((cut * columns + tile) * 2 + part) * height
                    skip = (side if cut == 0 else 1 - side) * height if owned_only else 0
                    first = tile * 2 * size + side * size + skip
                    rows = pl.ds(pl.multiple_of(first, height), height)
                    target[start : start + height, :] = grad[part, rows, :]


def whole_block(shape):
    return pl.BlockSpec(shape, lambda i, *_: (0,) * len(shape))


def prepared(place, positions, counts, measured):
    size = measured.shape[-1]
    slots = measured.shape[0] // 2
    order = np.zeros((size, size), ml_dtypes.bfloat16)
    order[np.concatenate([np.arange(0, size, 2), np.arange(1, size, 2)]), np.arange(size)] = 1
    return pl.pallas_call(
        prepare_kernel,
        out_shape=[
            jax.ShapeDtypeStruct((slots, size, size), jnp.float32),
            jax.ShapeDtypeStruct((4 * slots + 2,), jnp.int32),
        ],
        grid_spec=pltpu.PrefetchScalarGridSpec(
            num_scalar_prefetch=3,
            grid=(1,),
            in_specs=[
                pl.BlockSpec((slots, 1, size, size), lambda i, s, *_: (0, s[0], 0, 0)),
                whole_block((size, size)),
            ],
            out_specs=[
                whole_block((slots, size, size)),
                pl.BlockSpec(memory_space=pltpu.SMEM),
            ],
            scratch_shapes=[pltpu.VMEM((slots * size, size), jnp.float32)],
        ),
        compiler_params=pltpu.CompilerParams(vmem_limit_bytes=VMEM_LIMIT),
        cost_estimate=pl.CostEstimate(
            flops=6 * slots * size**3, bytes_accessed=8 * slots * size**2, transcendentals=0
        ),
        name="prepared",
    )(
        place,
        positions,
        counts,
        measured.reshape(slots, 2, size, size),
        jnp.asarray(order),
    )


def waves(windows, mine, theirs, root):
    slots, size, _ = root.shape
    columns = mine[0].shape[0] // (2 * size)
    group = slots if slots <= 8 else math.gcd(slots, 4)
    pair = (2 * size, size)
    pieces = (slots, 2, size, size)
    tables = [jnp.asarray(t) for t in transform_tables(size)]

    def body(*refs):
        wave_kernel(*refs, columns=columns, group=group)

    return pl.pallas_call(
        body,
        out_shape=[jax.ShapeDtypeStruct(s, jnp.float32) for s in (pair, pair, pieces)],
        grid_spec=pltpu.PrefetchScalarGridSpec(
            num_scalar_prefetch=1,
            grid=(1,),
            in_specs=[whole_block(mine[0].shape), whole_block(pair)] * 2
            + [whole_block(root.shape)]
            + [whole_block(t.shape) for t in tables],
            out_specs=[whole_block(s) for s in (pair, pair, pieces)],
            scratch_shapes=[
                pltpu.VMEM((2, columns * 2 * size, size), jnp.float32),
                pltpu.VMEM((2,) + pair, jnp.float32),
                pltpu.VMEM((2,) + pair, jnp.float32),
            ],
        ),
        compiler_params=pltpu.CompilerParams(vmem_limit_bytes=VMEM_LIMIT),
        name="waves",
    )(windows, *mine, *theirs, root, *tables)


def placed(windows, pieces, columns, owned_only):
    size = pieces.shape[-1]
    shape = (columns * 2 * size, size)

    def body(*refs):
        place_kernel(*refs, columns=columns, owned_only=owned_only)

    return pl.pallas_call(
        body,
        out_shape=[jax.ShapeDtypeStruct(shape, jnp.float32)] * 2,
        grid_spec=pltpu.PrefetchScalarGridSpec(
            num_scalar_prefetch=1,
            grid=(1,),
            in_specs=[whole_block(pieces.shape)],
            out_specs=[whole_block(shape)] * 2,
            scratch_shapes=[pltpu.VMEM((2,) + shape, jnp.float32)],
        ),
        compiler_params=pltpu.CompilerParams(vmem_limit_bytes=VMEM_LIMIT),
        name="placed",
    )(windows, pieces)


def swap_modes(block):
    return lax.ppermute(block, "mode", [(0, 1), (1, 0)])


def paired_with(index, parity, count):
    other = index + 1 if index % 2 == parity else index - 1
    return other if 0 <= other < count else None


def swap_neighbours(block, col_parity=None):
    rows, cols = lax.axis_size("row"), lax.axis_size("col")
    route = []
    for row in range(rows):
        for col in range(cols):
            for mode in range(2):
                to_row = paired_with(row, mode, rows)
                to_col = col if col_parity is None else paired_with(col, col_parity, cols)
                if to_col is None:
                    to_row, to_col = row, col
                elif to_row is None:
                    to_row = row
                    to_col = col ^ 1 if cols % 2 == 0 and col_parity is None else to_col
                route.append(
                    ((row * cols + col) * 2 + mode, (to_row * cols + to_col) * 2 + mode)
                )
    return lax.ppermute(block, ("row", "col", "mode"), route)


def from_cols(blocks, send):
    count = lax.axis_size("col")
    col = lax.axis_index("col")
    to_low, to_high = blocks
    from_low = from_high = jnp.zeros_like(to_low)
    for parity in range(min(2, count - 1)):
        is_low = col % 2 == parity
        got = send(jnp.where(is_low, to_high, to_low), parity)
        from_high = jnp.where(is_low & (col < count - 1), got, from_high)
        from_low = jnp.where(jnp.logical_not(is_low) & (col > 0), got, from_low)
    return from_low, from_high


def swap_cols(block, parity):
    count = lax.axis_size("col")
    others = [paired_with(i, parity, count) for i in range(count)]
    return lax.ppermute(block, "col", [(i, i if o is None else o) for i, o in enumerate(others)])


def tile_sum_stages(beside_little):
    rows, cols = lax.axis_size("row"), lax.axis_size("col")
    if beside_little and (rows, cols) == (4, 2):
        first = [[(0, 1)], [(2, 0), (1, 0), (3, 0)]]
        second = [[(2, 0)], [(0, 1), (1, 0), (1, 1)]]
    else:
        along_cols = [[(0, 1 << k)] for k in range((cols - 1).bit_length())]
        along_rows = [[(1 << k, 0)] for k in range((rows - 1).bit_length())]
        first = along_cols + along_rows
        second = along_rows + along_cols
        if len(along_rows) > 1:
            second = along_rows[1:2] + along_cols + along_rows[:1] + along_rows[2:]
    return [list(zip(*stage, strict=True)) for stage in zip(first, second, strict=True)]


def sum_tiles(block, stages):
    sums = []
    rows, cols = lax.axis_size("row"), lax.axis_size("col")
    for stage in stages:
        arrived = []
        for flips in stage:
            route = []
            for row in range(rows):
                for col in range(cols):
                    for mode in range(2):
                        to_row, to_col = row ^ flips[mode][0], col ^ flips[mode][1]
                        route.append(
                            ((row * cols + col) * 2 + mode, (to_row * cols + to_col) * 2 + mode)
                        )
            arrived.append(lax.ppermute(block, ("row", "col", "mode"), route))
        block = sum(arrived, start=block)
        sums.append(block)
    return sums


def on_device(obj, probe, positions, counts, measured):
    size = probe.shape[-1]
    half = size // 2
    tile_rows, tile_cols = obj.shape[1:]
    columns = tile_cols // size + 1
    slot_count = positions.shape[2]
    rows_count, cols_count = lax.axis_size("row"), lax.axis_size("col")
    me = lax.axis_index("mode")
    row = lax.axis_index("row")
    col = lax.axis_index("col")
    lower = row % 2 == me
    paired = jnp.where(lower, row < rows_count - 1, row > 0)
    half_mine = lower.astype(jnp.int32)
    place = jnp.stack(
        [me, half_mine, row * tile_rows - half, col * tile_cols - half]
    ).astype(jnp.int32)
    root, windows = prepared(place, positions[0, 0].T, counts, measured[0, 0])
    probe_step = probe_rate / (slot_count * rows_count * cols_count)

    strip = jnp.where(lower, obj[:, half:], obj[:, :half])
    edges = (strip[:, :, :half], strip[:, :, tile_cols - half :])
    beside = swap_neighbours(strip)
    strip_low, strip_high = from_cols(edges, swap_cols)
    corner_low, corner_high = from_cols(edges, swap_neighbours)
    beside, root, windows = lax.optimization_barrier((beside, root, windows))
    strip = jnp.concatenate([strip_low, strip, strip_high], axis=2)
    beside = jnp.concatenate([corner_low, beside, corner_high], axis=2)
    beside = jnp.where(paired, beside, 0.0)
    wide = jnp.concatenate(
        [jnp.where(lower, strip, beside), jnp.where(lower, beside, strip)], axis=1
    )
    tiles = [wide[:, :, tile * size : (tile + 1) * size] for tile in range(columns)]
    start = [
        jnp.concatenate(tiles).reshape(columns * 2 * size, size),
        probe[0].reshape(2 * size, size),
    ]

    ext_rows = jnp.arange(size, dtype=jnp.int32)[:, None] + half_mine * size - half
    ext_rows = jnp.concatenate([ext_rows, ext_rows]) + row * tile_rows
    rows_inside = (ext_rows >= 0) & (ext_rows < tile_rows * rows_count)
    rates = []
    for tile in range(columns):
        ext_cols = jnp.arange(size, dtype=jnp.int32)[None, :] + tile * size - half + col * tile_cols
        inside = rows_inside & (ext_cols >= 0) & (ext_cols < tile_cols * cols_count)
        rates.append(jnp.where(inside, jnp.float32(object_rate), 0.0))

    rates = jnp.concatenate(rates)
    previous, current = start, start
    ahead, others = start, [swap_modes(x) for x in start]
    for iteration in range(ITERS):
        keep, send, pieces = waves(windows, ahead, others, root)
        probe_grad = keep + swap_modes(send)
        keep, send = placed(windows, pieces, columns, iteration == ITERS - 1)
        probe_grad, keep, send = lax.optimization_barrier((probe_grad, keep, send))
        previous = current
        sums = sum_tiles(probe_grad, tile_sum_stages(iteration == ITERS - 1))
        probe_grad = sums[-1]
        object_grad = keep + swap_modes(send)
        if iteration < ITERS - 1:
            object_grad = object_grad + jnp.where(paired, swap_neighbours(object_grad), 0.0)
            object_grad, _ = lax.optimization_barrier((object_grad, sums[1]))
            parts = [
                object_grad[tile * 2 * size : (tile + 1) * 2 * size] for tile in range(columns)
            ]
            from_low, from_high = from_cols((parts[0], parts[-1]), swap_cols)
            parts[0] = parts[0] + from_low
            parts[-1] = parts[-1] + from_high
            new_object = ahead[0] - rates * jnp.concatenate(parts)
            probe_grad, new_object = lax.optimization_barrier((probe_grad, new_object))
            new_probe = ahead[1] - probe_step * probe_grad
            current = [new_object, new_probe]
            ahead = [x + momentum * (x - y) for x, y in zip(current, previous, strict=True)]
            others = [swap_modes(x) for x in ahead]
        else:
            object_grad = object_grad.reshape(2, columns, 2, half, size)
            given, owned = object_grad[0], object_grad[1]
            owned = owned + jnp.where(paired, swap_neighbours(given), 0.0)
            edges = (owned[0, :, :, :half], owned[-1, :, :, half:])
            from_low, from_high = from_cols(edges, swap_cols)
            owned = jnp.concatenate(
                [owned[0, :, :, half:] + from_low]
                + [owned[tile] for tile in range(1, columns - 1)]
                + [owned[-1, :, :, :half] + from_high],
                axis=2,
            )
            held = ahead[0].reshape(columns, 2, size, size)
            held = jnp.concatenate([held[tile] for tile in range(columns)], axis=2)
            held = jnp.where(lower, held[:, :half], held[:, half:])
            strip = held[:, :, half : half + tile_cols] - object_rate * owned

    other = swap_modes(strip)
    whole = jnp.concatenate(
        [jnp.where(lower, other, strip), jnp.where(lower, strip, other)], axis=1
    )
    probe_grad, _ = lax.optimization_barrier((probe_grad, whole))
    new_probe = ahead[-1] - probe_step * probe_grad
    return (whole, new_probe.reshape(1, 2, size, size))


def solution(mesh):
    in_specs = (
        P(None, ("parts", "row"), "col"),
        P("mode", None, "parts", None),
        P("row", "col", "parts", None),
        P(("parts", "row"), "col"),
        P("row", "col", "parts", None, None),
    )
    out_specs = (P(None, ("parts", "row"), "col"), P("mode", None, "parts", None))
    return jax.shard_map(
        on_device, mesh=mesh, in_specs=in_specs, out_specs=out_specs, check_vma=False
    )
```

```python
import math

import jax
import jax.numpy as jnp
import ml_dtypes
import numpy as np
from jax import lax
from jax.experimental import pallas as pl
from jax.experimental.pallas import tpu as pltpu
from jax.sharding import PartitionSpec as P

ITERS = 2


momentum = 0.5
object_rate = 0.1
probe_rate = 0.25

VMEM_LIMIT = 16 * 1024 * 1024


def transform_tables(size):
    half = size // 2
    point, freq = np.arange(half)[:, None], np.arange(half)[None, :]
    right, left, right_back, left_back = [], [], [], []
    for odd in range(2):
        angle = (point * (2 * freq + odd) % size) * (2.0 * np.pi / size)
        cosine, sine = np.cos(angle) / np.sqrt(size), np.sin(angle) / np.sqrt(size)
        table = np.block([[cosine, -sine], [sine, cosine]]).astype(np.float32)
        high = table.astype(ml_dtypes.bfloat16)
        low = (table - high.astype(np.float32)).astype(ml_dtypes.bfloat16)
        right.append(np.concatenate([high, low], axis=1))
        left.append(np.concatenate([high.T, low.T], axis=0))
        right_back.append(np.concatenate([high.T, low.T], axis=1))
        left_back.append(np.concatenate([high, low], axis=0))
    return [np.stack(t) for t in (right, left, left_back, right_back)]


def split(values):
    high = values.astype(jnp.bfloat16)
    return high, (values - high.astype(jnp.float32)).astype(jnp.bfloat16)


def matmul(left, right):
    return jnp.dot(left, right, preferred_element_type=jnp.float32)


def from_right(values, table):
    size = values.shape[1]
    both = matmul(
        jnp.concatenate(split(values), axis=1), jnp.concatenate([table, table], axis=0)
    )
    return both[:, :size] + both[:, size:]


def from_left(table, values):
    size = values.shape[0]
    both = matmul(
        jnp.concatenate([table, table], axis=1), jnp.concatenate(split(values), axis=0)
    )
    return both[:size] + both[size:]


def meld(first, second):
    half = first.shape[1] // 2
    low = lax.broadcasted_iota(jnp.int32, first.shape, 1) < half
    turned = pltpu.roll(jnp.where(low, second, first), half, 1)
    return jnp.where(low, first, turned), jnp.where(low, turned, second)


def stack_rows(*blocks):
    return jnp.concatenate(blocks, axis=0)


def stack_lanes(*blocks):
    return jnp.concatenate(blocks, axis=1)


def prepare_kernel(place, positions, counts, measured, order, root, windows, planes):
    slots, _, size, _ = measured.shape
    half = size // 2
    me = place[0]
    for index in range(slots):
        slot = 2 * index + me
        col = positions[1, slot] - place[3]
        windows[4 * index] = positions[0, slot] - place[2]
        windows[4 * index + 1] = col // size
        windows[4 * index + 2] = col % size
        windows[4 * index + 3] = (slot < counts[0, 0]).astype(jnp.int32)
    windows[4 * slots] = me
    windows[4 * slots + 1] = place[1]
    values = jnp.sqrt(measured[...].reshape(slots * size, size))
    high = values.astype(jnp.bfloat16)
    middle, low = split(values - high.astype(jnp.float32))
    planes[...] = matmul(high, order[...]) + (
        matmul(middle, order[...]) + matmul(low, order[...])
    )
    for index in range(slots):
        for odd in range(2):
            root[index, odd * half : (odd + 1) * half, :] = planes[
                pl.ds(index * size + odd, half, stride=2), :
            ]


def window_of(windows, index):
    return windows[4 * index], windows[4 * index + 1], windows[4 * index + 2]


def region(tile, half, size):
    return pl.ds(pl.multiple_of(tile * 2 * size + half * size, size), size)


def rows_of(row, tile, size):
    return pl.ds(tile * 2 * size + row, size)


def wave_kernel(windows, *refs, columns, group):
    mine, theirs = refs[:2], refs[2:4]
    root, right, left, left_back, right_back = refs[4:9]
    keep, send, pieces, state, modes, grad = refs[9:]
    slots, size, _ = root.shape
    half = size // 2
    me, half_mine = windows[4 * slots], windows[4 * slots + 1]
    lane = lax.broadcasted_iota(jnp.int32, (size, size), 1)

    for blocks, side, mode in ((mine, half_mine, me), (theirs, 1 - half_mine, 1 - me)):
        for part in range(2):
            for tile in range(columns):
                start = (2 * tile + part) * size
                state[part, region(tile, side, size), :] = blocks[0][start : start + size, :]
        modes[mode] = blocks[1][...]
    grad[...] = jnp.zeros_like(grad)

    def plane(mode, part):
        return modes[mode, part * size : (part + 1) * size, :]

    def one_group(first):
        patches, reals, imags = [], [], []
        for index in range(group):
            row, tile, shift = window_of(windows, first + index)
            patch = []
            for part in range(2):
                near = state[part, rows_of(row, tile, size), :]
                far = state[part, rows_of(row, tile + 1, size), :]
                patch.append(
                    pltpu.roll(jnp.where(lane >= shift, near, far), (size - shift) % size, 1)
                )
            patches.append(patch)
            for mode in range(2):
                real, imag = plane(mode, 0), plane(mode, 1)
                reals.append(real * patch[0] - imag * patch[1])
                imags.append(real * patch[1] + imag * patch[0])
        first_half, second_half = meld(stack_rows(*reals), stack_rows(*imags))
        real, imag = meld(
            from_right(first_half + second_half, right[0]),
            from_right(first_half - second_half, right[1]),
        )
        reals, imags = [], []
        for index in range(group):
            start = 2 * index * size
            both = [
                stack_lanes(x[start : start + size], x[start + size : start + 2 * size])
                for x in (real, imag)
            ]
            waves_back = []
            for odd in range(2):
                merged = [x[:half] - x[half:] if odd else x[:half] + x[half:] for x in both]
                far_field = from_left(left[odd], stack_rows(*merged))
                power = far_field * far_field
                power = power[:half] + power[half:]
                power = power[:, :size] + power[:, size:]
                live = windows[4 * (first + index) + 3].astype(jnp.float32)
                roots = root[first + index, odd * half : (odd + 1) * half, :]
                weight = (1.0 - roots * lax.rsqrt(power + 1.0)) * live
                weight = stack_lanes(weight, weight)
                waves_back.append(
                    from_left(left_back[odd], stack_rows(weight, weight) * far_field)
                )
            even, odd = waves_back
            sums, differences = even + odd, even - odd
            for mode in range(2):
                lanes = slice(mode * size, (mode + 1) * size)
                reals.append(stack_rows(sums[:half, lanes], differences[:half, lanes]))
                imags.append(stack_rows(sums[half:, lanes], differences[half:, lanes]))
        even, odd = meld(stack_rows(*reals), stack_rows(*imags))
        even, odd = from_right(even, right_back[0]), from_right(odd, right_back[1])
        real, imag = meld(even + odd, even - odd)
        for index in range(group):
            total = [0.0, 0.0]
            for mode in range(2):
                start = (2 * index + mode) * size
                chi_real, chi_imag = real[start : start + size], imag[start : start + size]
                probe_real, probe_imag = plane(mode, 0), plane(mode, 1)
                total[0] = total[0] + (probe_real * chi_real + probe_imag * chi_imag)
                total[1] = total[1] + (probe_real * chi_imag - probe_imag * chi_real)
                patch_real, patch_imag = patches[index]
                grad[mode, :size, :] += patch_real * chi_real + patch_imag * chi_imag
                grad[mode, size:, :] += patch_real * chi_imag - patch_imag * chi_real
            for part in range(2):
                pieces[first + index, part] = total[part]

    @pl.loop(0, slots // group)
    def _(step):
        one_group(step * group)

    keep[...] = grad[me]
    send[...] = grad[1 - me]


def place_kernel(windows, pieces, keep, send, grad, *, columns, owned_only):
    slots, _, size, _ = pieces.shape
    half_mine = windows[4 * slots + 1]
    lane = lax.broadcasted_iota(jnp.int32, (size, size), 1)
    grad[...] = jnp.zeros_like(grad)
    for index in range(slots):
        row, tile, shift = window_of(windows, index)
        inside = lane >= shift
        for part in range(2):
            turned = pltpu.roll(pieces[index, part], shift, 1)
            grad[part, rows_of(row, tile, size), :] += jnp.where(inside, turned, 0.0)
            grad[part, rows_of(row, tile + 1, size), :] += jnp.where(inside, 0.0, turned)
    cuts = 2 if owned_only else 1
    height = size // cuts
    for target, side in ((keep, half_mine), (send, 1 - half_mine)):
        for cut in range(cuts):
            for tile in range(columns):
                for part in range(2):
                    start = ((cut * columns + tile) * 2 + part) * height
                    skip = (side if cut == 0 else 1 - side) * height if owned_only else 0
                    first = tile * 2 * size + side * size + skip
                    rows = pl.ds(pl.multiple_of(first, height), height)
                    target[start : start + height, :] = grad[part, rows, :]


def whole_block(shape):
    return pl.BlockSpec(shape, lambda i, *_: (0,) * len(shape))


def prepared(place, positions, counts, measured):
    size = measured.shape[-1]
    slots = measured.shape[0] // 2
    order = np.zeros((size, size), ml_dtypes.bfloat16)
    order[np.concatenate([np.arange(0, size, 2), np.arange(1, size, 2)]), np.arange(size)] = 1
    return pl.pallas_call(
        prepare_kernel,
        out_shape=[
            jax.ShapeDtypeStruct((slots, size, size), jnp.float32),
            jax.ShapeDtypeStruct((4 * slots + 2,), jnp.int32),
        ],
        grid_spec=pltpu.PrefetchScalarGridSpec(
            num_scalar_prefetch=3,
            grid=(1,),
            in_specs=[
                pl.BlockSpec((slots, 1, size, size), lambda i, s, *_: (0, s[0], 0, 0)),
                whole_block((size, size)),
            ],
            out_specs=[
                whole_block((slots, size, size)),
                pl.BlockSpec(memory_space=pltpu.SMEM),
            ],
            scratch_shapes=[pltpu.VMEM((slots * size, size), jnp.float32)],
        ),
        compiler_params=pltpu.CompilerParams(vmem_limit_bytes=VMEM_LIMIT),
        cost_estimate=pl.CostEstimate(
            flops=6 * slots * size**3, bytes_accessed=8 * slots * size**2, transcendentals=0
        ),
        name="prepared",
    )(
        place,
        positions,
        counts,
        measured.reshape(slots, 2, size, size),
        jnp.asarray(order),
    )


def waves(windows, mine, theirs, root):
    slots, size, _ = root.shape
    columns = mine[0].shape[0] // (2 * size)
    group = slots if slots <= 8 else math.gcd(slots, 4)
    pair = (2 * size, size)
    pieces = (slots, 2, size, size)
    tables = [jnp.asarray(t) for t in transform_tables(size)]

    def body(*refs):
        wave_kernel(*refs, columns=columns, group=group)

    return pl.pallas_call(
        body,
        out_shape=[jax.ShapeDtypeStruct(s, jnp.float32) for s in (pair, pair, pieces)],
        grid_spec=pltpu.PrefetchScalarGridSpec(
            num_scalar_prefetch=1,
            grid=(1,),
            in_specs=[whole_block(mine[0].shape), whole_block(pair)] * 2
            + [whole_block(root.shape)]
            + [whole_block(t.shape) for t in tables],
            out_specs=[whole_block(s) for s in (pair, pair, pieces)],
            scratch_shapes=[
                pltpu.VMEM((2, columns * 2 * size, size), jnp.float32),
                pltpu.VMEM((2,) + pair, jnp.float32),
                pltpu.VMEM((2,) + pair, jnp.float32),
            ],
        ),
        compiler_params=pltpu.CompilerParams(vmem_limit_bytes=VMEM_LIMIT),
        name="waves",
    )(windows, *mine, *theirs, root, *tables)


def placed(windows, pieces, columns, owned_only):
    size = pieces.shape[-1]
    shape = (columns * 2 * size, size)

    def body(*refs):
        place_kernel(*refs, columns=columns, owned_only=owned_only)

    return pl.pallas_call(
        body,
        out_shape=[jax.ShapeDtypeStruct(shape, jnp.float32)] * 2,
        grid_spec=pltpu.PrefetchScalarGridSpec(
            num_scalar_prefetch=1,
            grid=(1,),
            in_specs=[whole_block(pieces.shape)],
            out_specs=[whole_block(shape)] * 2,
            scratch_shapes=[pltpu.VMEM((2,) + shape, jnp.float32)],
        ),
        compiler_params=pltpu.CompilerParams(vmem_limit_bytes=VMEM_LIMIT),
        name="placed",
    )(windows, pieces)


def swap_modes(block):
    return lax.ppermute(block, "mode", [(0, 1), (1, 0)])


def paired_with(index, parity, count):
    other = index + 1 if index % 2 == parity else index - 1
    return other if 0 <= other < count else None


def swap_neighbours(block, col_parity=None):
    rows, cols = lax.axis_size("row"), lax.axis_size("col")
    route = []
    for row in range(rows):
        for col in range(cols):
            for mode in range(2):
                to_row = paired_with(row, mode, rows)
                to_col = col if col_parity is None else paired_with(col, col_parity, cols)
                if to_col is None:
                    to_row, to_col = row, col
                elif to_row is None:
                    to_row = row
                    to_col = col ^ 1 if cols % 2 == 0 and col_parity is None else to_col
                route.append(
                    ((row * cols + col) * 2 + mode, (to_row * cols + to_col) * 2 + mode)
                )
    return lax.ppermute(block, ("row", "col", "mode"), route)


def from_cols(blocks, send):
    count = lax.axis_size("col")
    col = lax.axis_index("col")
    to_low, to_high = blocks
    from_low = from_high = jnp.zeros_like(to_low)
    for parity in range(min(2, count - 1)):
        is_low = col % 2 == parity
        got = send(jnp.where(is_low, to_high, to_low), parity)
        from_high = jnp.where(is_low & (col < count - 1), got, from_high)
        from_low = jnp.where(jnp.logical_not(is_low) & (col > 0), got, from_low)
    return from_low, from_high


def swap_cols(block, parity):
    count = lax.axis_size("col")
    others = [paired_with(i, parity, count) for i in range(count)]
    return lax.ppermute(block, "col", [(i, i if o is None else o) for i, o in enumerate(others)])


def tile_sum_stages(beside_little):
    rows, cols = lax.axis_size("row"), lax.axis_size("col")
    if beside_little and (rows, cols) == (4, 2):
        first = [[(0, 1)], [(3, 0), (2, 0), (1, 0)]]
        second = [[(2, 0)], [(1, 1), (1, 0), (0, 1)]]
    else:
        along_cols = [[(0, 1 << k)] for k in range((cols - 1).bit_length())]
        along_rows = [[(1 << k, 0)] for k in range((rows - 1).bit_length())]
        first = along_cols + along_rows
        second = along_rows + along_cols
        if len(along_rows) > 1:
            second = along_rows[1:2] + along_cols + along_rows[:1] + along_rows[2:]
    return [list(zip(*stage, strict=True)) for stage in zip(first, second, strict=True)]


def sum_tiles(block, stages):
    sums = []
    rows, cols = lax.axis_size("row"), lax.axis_size("col")
    for stage in stages:
        arrived = []
        for flips in stage:
            route = []
            for row in range(rows):
                for col in range(cols):
                    for mode in range(2):
                        to_row, to_col = row ^ flips[mode][0], col ^ flips[mode][1]
                        route.append(
                            ((row * cols + col) * 2 + mode, (to_row * cols + to_col) * 2 + mode)
                        )
            arrived.append(lax.ppermute(block, ("row", "col", "mode"), route))
        block = sum(arrived, start=block)
        sums.append(block)
    return sums


def on_device(obj, probe, positions, counts, measured):
    size = probe.shape[-1]
    half = size // 2
    tile_rows, tile_cols = obj.shape[1:]
    columns = tile_cols // size + 1
    slot_count = positions.shape[2]
    rows_count, cols_count = lax.axis_size("row"), lax.axis_size("col")
    me = lax.axis_index("mode")
    row = lax.axis_index("row")
    col = lax.axis_index("col")
    lower = row % 2 == me
    paired = jnp.where(lower, row < rows_count - 1, row > 0)
    half_mine = lower.astype(jnp.int32)
    place = jnp.stack(
        [me, half_mine, row * tile_rows - half, col * tile_cols - half]
    ).astype(jnp.int32)
    root, windows = prepared(place, positions[0, 0].T, counts, measured[0, 0])
    probe_step = probe_rate / (slot_count * rows_count * cols_count)

    strip = jnp.where(lower, obj[:, half:], obj[:, :half])
    edges = (strip[:, :, :half], strip[:, :, tile_cols - half :])
    beside = swap_neighbours(strip)
    strip_low, strip_high = from_cols(edges, swap_cols)
    corner_low, corner_high = from_cols(edges, swap_neighbours)
    beside, root, windows = lax.optimization_barrier((beside, root, windows))
    strip = jnp.concatenate([strip_low, strip, strip_high], axis=2)
    beside = jnp.concatenate([corner_low, beside, corner_high], axis=2)
    beside = jnp.where(paired, beside, 0.0)
    wide = jnp.concatenate(
        [jnp.where(lower, strip, beside), jnp.where(lower, beside, strip)], axis=1
    )
    tiles = [wide[:, :, tile * size : (tile + 1) * size] for tile in range(columns)]
    start = [
        jnp.concatenate(tiles).reshape(columns * 2 * size, size),
        probe[0].reshape(2 * size, size),
    ]

    ext_rows = jnp.arange(size, dtype=jnp.int32)[:, None] + half_mine * size - half
    ext_rows = jnp.concatenate([ext_rows, ext_rows]) + row * tile_rows
    rows_inside = (ext_rows >= 0) & (ext_rows < tile_rows * rows_count)
    rates = []
    for tile in range(columns):
        ext_cols = jnp.arange(size, dtype=jnp.int32)[None, :] + tile * size - half + col * tile_cols
        inside = rows_inside & (ext_cols >= 0) & (ext_cols < tile_cols * cols_count)
        rates.append(jnp.where(inside, jnp.float32(object_rate), 0.0))

    rates = jnp.concatenate(rates)
    previous, current = start, start
    ahead, others = start, [swap_modes(x) for x in start]
    for iteration in range(ITERS):
        keep, send, pieces = waves(windows, ahead, others, root)
        probe_grad = keep + swap_modes(send)
        keep, send = placed(windows, pieces, columns, iteration == ITERS - 1)
        probe_grad, keep, send = lax.optimization_barrier((probe_grad, keep, send))
        previous = current
        sums = sum_tiles(probe_grad, tile_sum_stages(iteration == ITERS - 1))
        probe_grad = sums[-1]
        object_grad = keep + swap_modes(send)
        if iteration < ITERS - 1:
            object_grad = object_grad + jnp.where(paired, swap_neighbours(object_grad), 0.0)
            object_grad, _ = lax.optimization_barrier((object_grad, sums[1]))
            parts = [
                object_grad[tile * 2 * size : (tile + 1) * 2 * size] for tile in range(columns)
            ]
            from_low, from_high = from_cols((parts[0], parts[-1]), swap_cols)
            parts[0] = parts[0] + from_low
            parts[-1] = parts[-1] + from_high
            new_object = ahead[0] - rates * jnp.concatenate(parts)
            probe_grad, new_object = lax.optimization_barrier((probe_grad, new_object))
            new_probe = ahead[1] - probe_step * probe_grad
            current = [new_object, new_probe]
            ahead = [x + momentum * (x - y) for x, y in zip(current, previous, strict=True)]
            others = [swap_modes(x) for x in ahead]
        else:
            object_grad = object_grad.reshape(2, columns, 2, half, size)
            given, owned = object_grad[0], object_grad[1]
            owned = owned + jnp.where(paired, swap_neighbours(given), 0.0)
            edges = (owned[0, :, :, :half], owned[-1, :, :, half:])
            from_low, from_high = from_cols(edges, swap_cols)
            owned = jnp.concatenate(
                [owned[0, :, :, half:] + from_low]
                + [owned[tile] for tile in range(1, columns - 1)]
                + [owned[-1, :, :, :half] + from_high],
                axis=2,
            )
            held = ahead[0].reshape(columns, 2, size, size)
            held = jnp.concatenate([held[tile] for tile in range(columns)], axis=2)
            held = jnp.where(lower, held[:, :half], held[:, half:])
            strip = held[:, :, half : half + tile_cols] - object_rate * owned

    other = swap_modes(strip)
    whole = jnp.concatenate(
        [jnp.where(lower, other, strip), jnp.where(lower, strip, other)], axis=1
    )
    probe_grad, _ = lax.optimization_barrier((probe_grad, whole))
    new_probe = ahead[-1] - probe_step * probe_grad
    return (whole, new_probe.reshape(1, 2, size, size))


def solution(mesh):
    in_specs = (
        P(None, ("parts", "row"), "col"),
        P("mode", None, "parts", None),
        P("row", "col", "parts", None),
        P(("parts", "row"), "col"),
        P("row", "col", "parts", None, None),
    )
    out_specs = (P(None, ("parts", "row"), "col"), P("mode", None, "parts", None))
    return jax.shard_map(
        on_device, mesh=mesh, in_specs=in_specs, out_specs=out_specs, check_vma=False
    )
```

```python
import math

import jax
import jax.numpy as jnp
import ml_dtypes
import numpy as np
from jax import lax
from jax.experimental import pallas as pl
from jax.experimental.pallas import tpu as pltpu
from jax.sharding import PartitionSpec as P

ITERS = 2


momentum = 0.5
object_rate = 0.1
probe_rate = 0.25

VMEM_LIMIT = 16 * 1024 * 1024


def transform_tables(size):
    half = size // 2
    point, freq = np.arange(half)[:, None], np.arange(half)[None, :]
    right, left, right_back, left_back = [], [], [], []
    for odd in range(2):
        angle = (point * (2 * freq + odd) % size) * (2.0 * np.pi / size)
        cosine, sine = np.cos(angle) / np.sqrt(size), np.sin(angle) / np.sqrt(size)
        table = np.block([[cosine, -sine], [sine, cosine]]).astype(np.float32)
        high = table.astype(ml_dtypes.bfloat16)
        low = (table - high.astype(np.float32)).astype(ml_dtypes.bfloat16)
        right.append(np.concatenate([high, low], axis=1))
        left.append(np.concatenate([high.T, low.T], axis=0))
        right_back.append(np.concatenate([high.T, low.T], axis=1))
        left_back.append(np.concatenate([high, low], axis=0))
    return [np.stack(t) for t in (right, left, left_back, right_back)]


def split(values):
    high = values.astype(jnp.bfloat16)
    return high, (values - high.astype(jnp.float32)).astype(jnp.bfloat16)


def matmul(left, right):
    return jnp.dot(left, right, preferred_element_type=jnp.float32)


def from_right(values, table):
    size = values.shape[1]
    both = matmul(
        jnp.concatenate(split(values), axis=1), jnp.concatenate([table, table], axis=0)
    )
    return both[:, :size] + both[:, size:]


def from_left(table, values):
    size = values.shape[0]
    both = matmul(
        jnp.concatenate([table, table], axis=1), jnp.concatenate(split(values), axis=0)
    )
    return both[:size] + both[size:]


def meld(first, second):
    half = first.shape[1] // 2
    low = lax.broadcasted_iota(jnp.int32, first.shape, 1) < half
    turned = pltpu.roll(jnp.where(low, second, first), half, 1)
    return jnp.where(low, first, turned), jnp.where(low, turned, second)


def stack_rows(*blocks):
    return jnp.concatenate(blocks, axis=0)


def stack_lanes(*blocks):
    return jnp.concatenate(blocks, axis=1)


def prepare_kernel(place, positions, counts, measured, order, root, windows, planes):
    slots, _, size, _ = measured.shape
    half = size // 2
    me = place[0]
    for index in range(slots):
        slot = 2 * index + me
        col = positions[1, slot] - place[3]
        windows[4 * index] = positions[0, slot] - place[2]
        windows[4 * index + 1] = col // size
        windows[4 * index + 2] = col % size
        windows[4 * index + 3] = (slot < counts[0, 0]).astype(jnp.int32)
    windows[4 * slots] = me
    windows[4 * slots + 1] = place[1]
    values = jnp.sqrt(measured[...].reshape(slots * size, size))
    high = values.astype(jnp.bfloat16)
    middle, low = split(values - high.astype(jnp.float32))
    planes[...] = matmul(high, order[...]) + (
        matmul(middle, order[...]) + matmul(low, order[...])
    )
    for index in range(slots):
        for odd in range(2):
            root[index, odd * half : (odd + 1) * half, :] = planes[
                pl.ds(index * size + odd, half, stride=2), :
            ]


def window_of(windows, index):
    return windows[4 * index], windows[4 * index + 1], windows[4 * index + 2]


def region(tile, half, size):
    return pl.ds(pl.multiple_of(tile * 2 * size + half * size, size), size)


def rows_of(row, tile, size):
    return pl.ds(tile * 2 * size + row, size)


def wave_kernel(windows, *refs, columns, group):
    mine, theirs = refs[:2], refs[2:4]
    root, right, left, left_back, right_back = refs[4:9]
    keep, send, pieces, state, modes, grad = refs[9:]
    slots, size, _ = root.shape
    half = size // 2
    me, half_mine = windows[4 * slots], windows[4 * slots + 1]
    lane = lax.broadcasted_iota(jnp.int32, (size, size), 1)

    for blocks, side, mode in ((mine, half_mine, me), (theirs, 1 - half_mine, 1 - me)):
        for part in range(2):
            for tile in range(columns):
                start = (2 * tile + part) * size
                state[part, region(tile, side, size), :] = blocks[0][start : start + size, :]
        modes[mode] = blocks[1][...]
    grad[...] = jnp.zeros_like(grad)

    def plane(mode, part):
        return modes[mode, part * size : (part + 1) * size, :]

    def one_group(first):
        patches, reals, imags = [], [], []
        for index in range(group):
            row, tile, shift = window_of(windows, first + index)
            patch = []
            for part in range(2):
                near = state[part, rows_of(row, tile, size), :]
                far = state[part, rows_of(row, tile + 1, size), :]
                patch.append(
                    pltpu.roll(jnp.where(lane >= shift, near, far), (size - shift) % size, 1)
                )
            patches.append(patch)
            for mode in range(2):
                real, imag = plane(mode, 0), plane(mode, 1)
                reals.append(real * patch[0] - imag * patch[1])
                imags.append(real * patch[1] + imag * patch[0])
        first_half, second_half = meld(stack_rows(*reals), stack_rows(*imags))
        real, imag = meld(
            from_right(first_half + second_half, right[0]),
            from_right(first_half - second_half, right[1]),
        )
        reals, imags = [], []
        for index in range(group):
            start = 2 * index * size
            both = [
                stack_lanes(x[start : start + size], x[start + size : start + 2 * size])
                for x in (real, imag)
            ]
            waves_back = []
            for odd in range(2):
                merged = [x[:half] - x[half:] if odd else x[:half] + x[half:] for x in both]
                far_field = from_left(left[odd], stack_rows(*merged))
                power = far_field * far_field
                power = power[:half] + power[half:]
                power = power[:, :size] + power[:, size:]
                live = windows[4 * (first + index) + 3].astype(jnp.float32)
                roots = root[first + index, odd * half : (odd + 1) * half, :]
                weight = (1.0 - roots * lax.rsqrt(power + 1.0)) * live
                weight = stack_lanes(weight, weight)
                waves_back.append(
                    from_left(left_back[odd], stack_rows(weight, weight) * far_field)
                )
            even, odd = waves_back
            sums, differences = even + odd, even - odd
            for mode in range(2):
                lanes = slice(mode * size, (mode + 1) * size)
                reals.append(stack_rows(sums[:half, lanes], differences[:half, lanes]))
                imags.append(stack_rows(sums[half:, lanes], differences[half:, lanes]))
        even, odd = meld(stack_rows(*reals), stack_rows(*imags))
        even, odd = from_right(even, right_back[0]), from_right(odd, right_back[1])
        real, imag = meld(even + odd, even - odd)
        for index in range(group):
            total = [0.0, 0.0]
            for mode in range(2):
                start = (2 * index + mode) * size
                chi_real, chi_imag = real[start : start + size], imag[start : start + size]
                probe_real, probe_imag = plane(mode, 0), plane(mode, 1)
                total[0] = total[0] + (probe_real * chi_real + probe_imag * chi_imag)
                total[1] = total[1] + (probe_real * chi_imag - probe_imag * chi_real)
                patch_real, patch_imag = patches[index]
                grad[mode, :size, :] += patch_real * chi_real + patch_imag * chi_imag
                grad[mode, size:, :] += patch_real * chi_imag - patch_imag * chi_real
            for part in range(2):
                pieces[first + index, part] = total[part]

    @pl.loop(0, slots // group)
    def _(step):
        one_group(step * group)

    keep[...] = grad[me]
    send[...] = grad[1 - me]


def place_kernel(windows, pieces, keep, send, grad, *, columns, owned_only):
    slots, _, size, _ = pieces.shape
    half_mine = windows[4 * slots + 1]
    lane = lax.broadcasted_iota(jnp.int32, (size, size), 1)
    grad[...] = jnp.zeros_like(grad)
    for index in range(slots):
        row, tile, shift = window_of(windows, index)
        inside = lane >= shift
        for part in range(2):
            turned = pltpu.roll(pieces[index, part], shift, 1)
            grad[part, rows_of(row, tile, size), :] += jnp.where(inside, turned, 0.0)
            grad[part, rows_of(row, tile + 1, size), :] += jnp.where(inside, 0.0, turned)
    cuts = 2 if owned_only else 1
    height = size // cuts
    for target, side in ((keep, half_mine), (send, 1 - half_mine)):
        for cut in range(cuts):
            for tile in range(columns):
                for part in range(2):
                    start = ((cut * columns + tile) * 2 + part) * height
                    skip = (side if cut == 0 else 1 - side) * height if owned_only else 0
                    first = tile * 2 * size + side * size + skip
                    rows = pl.ds(pl.multiple_of(first, height), height)
                    target[start : start + height, :] = grad[part, rows, :]


def whole_block(shape):
    return pl.BlockSpec(shape, lambda i, *_: (0,) * len(shape))


def prepared(place, positions, counts, measured):
    size = measured.shape[-1]
    slots = measured.shape[0] // 2
    order = np.zeros((size, size), ml_dtypes.bfloat16)
    order[np.concatenate([np.arange(0, size, 2), np.arange(1, size, 2)]), np.arange(size)] = 1
    return pl.pallas_call(
        prepare_kernel,
        out_shape=[
            jax.ShapeDtypeStruct((slots, size, size), jnp.float32),
            jax.ShapeDtypeStruct((4 * slots + 2,), jnp.int32),
        ],
        grid_spec=pltpu.PrefetchScalarGridSpec(
            num_scalar_prefetch=3,
            grid=(1,),
            in_specs=[
                pl.BlockSpec((slots, 1, size, size), lambda i, s, *_: (0, s[0], 0, 0)),
                whole_block((size, size)),
            ],
            out_specs=[
                whole_block((slots, size, size)),
                pl.BlockSpec(memory_space=pltpu.SMEM),
            ],
            scratch_shapes=[pltpu.VMEM((slots * size, size), jnp.float32)],
        ),
        compiler_params=pltpu.CompilerParams(vmem_limit_bytes=VMEM_LIMIT),
        cost_estimate=pl.CostEstimate(
            flops=6 * slots * size**3, bytes_accessed=8 * slots * size**2, transcendentals=0
        ),
        name="prepared",
    )(
        place,
        positions,
        counts,
        measured.reshape(slots, 2, size, size),
        jnp.asarray(order),
    )


def waves(windows, mine, theirs, root):
    slots, size, _ = root.shape
    columns = mine[0].shape[0] // (2 * size)
    group = slots if slots <= 8 else math.gcd(slots, 4)
    pair = (2 * size, size)
    pieces = (slots, 2, size, size)
    tables = [jnp.asarray(t) for t in transform_tables(size)]

    def body(*refs):
        wave_kernel(*refs, columns=columns, group=group)

    return pl.pallas_call(
        body,
        out_shape=[jax.ShapeDtypeStruct(s, jnp.float32) for s in (pair, pair, pieces)],
        grid_spec=pltpu.PrefetchScalarGridSpec(
            num_scalar_prefetch=1,
            grid=(1,),
            in_specs=[whole_block(mine[0].shape), whole_block(pair)] * 2
            + [whole_block(root.shape)]
            + [whole_block(t.shape) for t in tables],
            out_specs=[whole_block(s) for s in (pair, pair, pieces)],
            scratch_shapes=[
                pltpu.VMEM((2, columns * 2 * size, size), jnp.float32),
                pltpu.VMEM((2,) + pair, jnp.float32),
                pltpu.VMEM((2,) + pair, jnp.float32),
            ],
        ),
        compiler_params=pltpu.CompilerParams(vmem_limit_bytes=VMEM_LIMIT),
        name="waves",
    )(windows, *mine, *theirs, root, *tables)


def placed(windows, pieces, columns, owned_only):
    size = pieces.shape[-1]
    shape = (columns * 2 * size, size)

    def body(*refs):
        place_kernel(*refs, columns=columns, owned_only=owned_only)

    return pl.pallas_call(
        body,
        out_shape=[jax.ShapeDtypeStruct(shape, jnp.float32)] * 2,
        grid_spec=pltpu.PrefetchScalarGridSpec(
            num_scalar_prefetch=1,
            grid=(1,),
            in_specs=[whole_block(pieces.shape)],
            out_specs=[whole_block(shape)] * 2,
            scratch_shapes=[pltpu.VMEM((2,) + shape, jnp.float32)],
        ),
        compiler_params=pltpu.CompilerParams(vmem_limit_bytes=VMEM_LIMIT),
        name="placed",
    )(windows, pieces)


def swap_modes(block):
    return lax.ppermute(block, "mode", [(0, 1), (1, 0)])


def paired_with(index, parity, count):
    other = index + 1 if index % 2 == parity else index - 1
    return other if 0 <= other < count else None


def swap_neighbours(block, col_parity=None):
    rows, cols = lax.axis_size("row"), lax.axis_size("col")
    route = []
    for row in range(rows):
        for col in range(cols):
            for mode in range(2):
                to_row = paired_with(row, mode, rows)
                to_col = col if col_parity is None else paired_with(col, col_parity, cols)
                if to_col is None:
                    to_row, to_col = row, col
                elif to_row is None:
                    to_row = row
                    to_col = col ^ 1 if cols % 2 == 0 and col_parity is None else to_col
                route.append(
                    ((row * cols + col) * 2 + mode, (to_row * cols + to_col) * 2 + mode)
                )
    return lax.ppermute(block, ("row", "col", "mode"), route)


def from_cols(blocks, send):
    count = lax.axis_size("col")
    col = lax.axis_index("col")
    to_low, to_high = blocks
    from_low = from_high = jnp.zeros_like(to_low)
    for parity in range(min(2, count - 1)):
        is_low = col % 2 == parity
        got = send(jnp.where(is_low, to_high, to_low), parity)
        from_high = jnp.where(is_low & (col < count - 1), got, from_high)
        from_low = jnp.where(jnp.logical_not(is_low) & (col > 0), got, from_low)
    return from_low, from_high


def swap_cols(block, parity):
    count = lax.axis_size("col")
    others = [paired_with(i, parity, count) for i in range(count)]
    return lax.ppermute(block, "col", [(i, i if o is None else o) for i, o in enumerate(others)])


def tile_sum_stages(beside_little):
    rows, cols = lax.axis_size("row"), lax.axis_size("col")
    if beside_little and (rows, cols) == (4, 2):
        first = [[(0, 1)], [(3, 0), (2, 0), (1, 0)]]
        second = [[(2, 0)], [(1, 1), (1, 0), (0, 1)]]
    else:
        along_cols = [[(0, 1 << k)] for k in range((cols - 1).bit_length())]
        along_rows = [[(1 << k, 0)] for k in range((rows - 1).bit_length())]
        first = along_cols + along_rows
        second = along_rows + along_cols
        if len(along_rows) > 1:
            second = along_rows[1:2] + along_cols + along_rows[:1] + along_rows[2:]
    return [list(zip(*stage, strict=True)) for stage in zip(first, second, strict=True)]


def sum_tiles(block, stages):
    sums = []
    rows, cols = lax.axis_size("row"), lax.axis_size("col")
    for stage in stages:
        arrived = []
        for flips in stage:
            route = []
            for row in range(rows):
                for col in range(cols):
                    for mode in range(2):
                        to_row, to_col = row ^ flips[mode][0], col ^ flips[mode][1]
                        route.append(
                            ((row * cols + col) * 2 + mode, (to_row * cols + to_col) * 2 + mode)
                        )
            arrived.append(lax.ppermute(block, ("row", "col", "mode"), route))
        block = sum(arrived, start=block)
        sums.append(block)
    return sums


def on_device(obj, probe, positions, counts, measured):
    size = probe.shape[-1]
    half = size // 2
    tile_rows, tile_cols = obj.shape[1:]
    columns = tile_cols // size + 1
    slot_count = positions.shape[2]
    rows_count, cols_count = lax.axis_size("row"), lax.axis_size("col")
    me = lax.axis_index("mode")
    row = lax.axis_index("row")
    col = lax.axis_index("col")
    lower = row % 2 == me
    paired = jnp.where(lower, row < rows_count - 1, row > 0)
    half_mine = lower.astype(jnp.int32)
    place = jnp.stack(
        [me, half_mine, row * tile_rows - half, col * tile_cols - half]
    ).astype(jnp.int32)
    root, windows = prepared(place, positions[0, 0].T, counts, measured[0, 0])
    probe_step = probe_rate / (slot_count * rows_count * cols_count)

    strip = jnp.where(lower, obj[:, half:], obj[:, :half])
    edges = (strip[:, :, :half], strip[:, :, tile_cols - half :])
    strip, *edges = lax.optimization_barrier((strip, *edges))
    beside = swap_neighbours(strip)
    strip_low, strip_high = from_cols(edges, swap_cols)
    corner_low, corner_high = from_cols(edges, swap_neighbours)
    beside, root, windows = lax.optimization_barrier((beside, root, windows))
    strip = jnp.concatenate([strip_low, strip, strip_high], axis=2)
    beside = jnp.concatenate([corner_low, beside, corner_high], axis=2)
    beside = jnp.where(paired, beside, 0.0)
    wide = jnp.concatenate(
        [jnp.where(lower, strip, beside), jnp.where(lower, beside, strip)], axis=1
    )
    tiles = [wide[:, :, tile * size : (tile + 1) * size] for tile in range(columns)]
    start = [
        jnp.concatenate(tiles).reshape(columns * 2 * size, size),
        probe[0].reshape(2 * size, size),
    ]

    ext_rows = jnp.arange(size, dtype=jnp.int32)[:, None] + half_mine * size - half
    ext_rows = jnp.concatenate([ext_rows, ext_rows]) + row * tile_rows
    rows_inside = (ext_rows >= 0) & (ext_rows < tile_rows * rows_count)
    rates = []
    for tile in range(columns):
        ext_cols = jnp.arange(size, dtype=jnp.int32)[None, :] + tile * size - half + col * tile_cols
        inside = rows_inside & (ext_cols >= 0) & (ext_cols < tile_cols * cols_count)
        rates.append(jnp.where(inside, jnp.float32(object_rate), 0.0))

    rates = jnp.concatenate(rates)
    previous, current = start, start
    ahead, others = start, [swap_modes(x) for x in start]
    for iteration in range(ITERS):
        keep, send, pieces = waves(windows, ahead, others, root)
        probe_grad = keep + swap_modes(send)
        keep, send = placed(windows, pieces, columns, iteration == ITERS - 1)
        probe_grad, keep, send = lax.optimization_barrier((probe_grad, keep, send))
        previous = current
        sums = sum_tiles(probe_grad, tile_sum_stages(iteration == ITERS - 1))
        probe_grad = sums[-1]
        object_grad = keep + swap_modes(send)
        if iteration < ITERS - 1:
            object_grad = object_grad + jnp.where(paired, swap_neighbours(object_grad), 0.0)
            object_grad, _ = lax.optimization_barrier((object_grad, sums[1]))
            parts = [
                object_grad[tile * 2 * size : (tile + 1) * 2 * size] for tile in range(columns)
            ]
            from_low, from_high = from_cols((parts[0], parts[-1]), swap_cols)
            parts[0] = parts[0] + from_low
            parts[-1] = parts[-1] + from_high
            new_object = ahead[0] - rates * jnp.concatenate(parts)
            probe_grad, new_object = lax.optimization_barrier((probe_grad, new_object))
            new_probe = ahead[1] - probe_step * probe_grad
            current = [new_object, new_probe]
            ahead = [x + momentum * (x - y) for x, y in zip(current, previous, strict=True)]
            others = [swap_modes(x) for x in ahead]
        else:
            object_grad = object_grad.reshape(2, columns, 2, half, size)
            given, owned = object_grad[0], object_grad[1]
            owned = owned + jnp.where(paired, swap_neighbours(given), 0.0)
            edges = (owned[0, :, :, :half], owned[-1, :, :, half:])
            from_low, from_high = from_cols(edges, swap_cols)
            owned = jnp.concatenate(
                [owned[0, :, :, half:] + from_low]
                + [owned[tile] for tile in range(1, columns - 1)]
                + [owned[-1, :, :, :half] + from_high],
                axis=2,
            )
            held = ahead[0].reshape(columns, 2, size, size)
            held = jnp.concatenate([held[tile] for tile in range(columns)], axis=2)
            held = jnp.where(lower, held[:, :half], held[:, half:])
            strip = held[:, :, half : half + tile_cols] - object_rate * owned

    other = swap_modes(strip)
    whole = jnp.concatenate(
        [jnp.where(lower, other, strip), jnp.where(lower, strip, other)], axis=1
    )
    probe_grad, _ = lax.optimization_barrier((probe_grad, whole))
    new_probe = ahead[-1] - probe_step * probe_grad
    return (whole, new_probe.reshape(1, 2, size, size))


def solution(mesh):
    in_specs = (
        P(None, ("parts", "row"), "col"),
        P("mode", None, "parts", None),
        P("row", "col", "parts", None),
        P(("parts", "row"), "col"),
        P("row", "col", "parts", None, None),
    )
    out_specs = (P(None, ("parts", "row"), "col"), P("mode", None, "parts", None))
    return jax.shard_map(
        on_device, mesh=mesh, in_specs=in_specs, out_specs=out_specs, check_vma=False
    )
```
